32 devices in a mesh: rx: 4 (over y, x), ry: 8 (over z, core).
Axes of the slice: x: 2, y: 2, z: 4, core: 2. Of those that a mesh axis runs over, the one named last changes fastest.
Arguments:
- block_input: bfloat16 [4, 8, 4, 197, 768], P('rx', 'ry'), may hold values from -6 to 6
- out_cotangent: bfloat16 [4, 8, 4, 197, 768], P('rx', 'ry'), may hold values from -6 to 6
- w_qkv: bfloat16 [4, 8, 768, 2304], P('rx', 'ry'), may hold values from -6 to 6
- w_proj: bfloat16 [4, 8, 768, 768], P('rx', 'ry'), may hold values from -6 to 6
Outputs:
- new_qkv: bfloat16 [4, 8, 768, 2304], P('rx', 'ry')
- new_proj: bfloat16 [4, 8, 768, 768], P('rx', 'ry')
The draws below stay inside these ranges and needn't reach their ends.
All inputs are finite; a program needn't handle non-finite values.
Results may differ from the reference program's by a relative error of at most 0.0059.
Values may be sent and summed in bfloat16 or wider, within the bound.
No kernel may reach another device: no remote copies, remote signals or barrier semaphores. Data moves between devices by JAX's collectives and lax.ppermute only.
A program may use at most 192 MiB of HBM per device.

```python
import jax
import jax.numpy as jnp
from jax import lax

D = 768
HEADS = 12
SEQ = 197
IMG = 4
LR = 1
HEAD = 64
N_RX = 4
N_RY = 8


def draw_block_input(key, part):
    key = jax.random.fold_in(key, 11)
    entries = jax.random.normal(key, (N_RX, N_RY, IMG, SEQ, D), jnp.float32)
    return jnp.clip(entries, -6.0, 6.0).astype(jnp.bfloat16)


def draw_w_qkv(key, part):
    key = jax.random.fold_in(key, 12)
    entries = jax.random.normal(key, (N_RX, N_RY, D, 3 * D), jnp.float32)
    return jnp.clip(entries, -6.0, 6.0).astype(jnp.bfloat16)


def block_scale(own_key, shape, cuts, smallest, largest):
    gain = 1.0
    for axis_at, parts in cuts:
        heights = jax.random.uniform(jax.random.fold_in(jax.random.fold_in(own_key, 6), axis_at), (parts,), jnp.float32, smallest / len(cuts), largest / len(cuts))
        gain = gain * jnp.repeat(jnp.exp(heights), shape[axis_at] // parts).reshape((-1,) + (1,) * (len(shape) - 1 - axis_at))
    return gain


def gaussian(stream_key, dims, width, reach, shards=(), held_as=jnp.bfloat16):
    level = block_scale(stream_key, dims, shards, -0.22, 0.18) if shards else 1.0
    drawn = jax.random.normal(stream_key, dims, jnp.float32) * width * level
    return jnp.minimum(jnp.maximum(drawn, -reach), reach).astype(held_as)


def setup_inputs(seed: int = 0) -> dict:
    seeds = jax.random.split(jax.random.key(seed), 5)
    return {
        "block_input": draw_block_input(jax.random.fold_in(seeds[4], 71), 0),
        "out_cotangent": gaussian(seeds[1], (N_RX, N_RY, IMG, SEQ, D), 1.0, 6.0, ((0, 4), (1, 8))),
        "w_qkv": draw_w_qkv(jax.random.fold_in(seeds[4], 71), 0),
        "w_proj": gaussian(seeds[3], (N_RX, N_RY, D, D), 1.0, 6.0, ((0, 4), (1, 8))),
    }


def replica_grads(packed):
    tokens, cotangent, w_qkv, w_proj = packed
    f32 = jnp.float32
    bf16 = jnp.bfloat16
    scale = D ** (-0.5)
    hscale = HEAD ** (-0.5)
    xf = tokens.astype(f32)
    mean = lax.optimization_barrier(jnp.mean(xf, axis=-1, keepdims=True))
    var = lax.optimization_barrier(jnp.mean((xf - mean) ** 2, axis=-1, keepdims=True))
    normed = ((xf - mean) * lax.rsqrt(var + 1e-06)).astype(bf16)
    qkv = (jnp.einsum('btd,de->bte', normed.astype(f32), w_qkv.astype(f32)) * scale).astype(bf16)
    query = qkv[:, :, :D].reshape(IMG, SEQ, HEADS, HEAD)
    keys = qkv[:, :, D:2 * D].reshape(IMG, SEQ, HEADS, HEAD)
    values = qkv[:, :, 2 * D:].reshape(IMG, SEQ, HEADS, HEAD)
    scores = jnp.einsum('bqhe,bkhe->bhqk', query.astype(f32), keys.astype(f32)) * hscale
    probs = jax.nn.softmax(scores, axis=-1)
    probs_b = probs.astype(bf16)
    attended = jnp.einsum('bhqk,bkhe->bqhe', probs_b.astype(f32), values.astype(f32)).astype(bf16)
    attended = attended.reshape(IMG, SEQ, D)
    grad_proj = jnp.einsum('btd,bte->de', attended.astype(f32), cotangent.astype(f32)) * scale
    d_att = (jnp.einsum('bte,de->btd', cotangent.astype(f32), w_proj.astype(f32)) * scale).astype(bf16)
    d_att = d_att.reshape(IMG, SEQ, HEADS, HEAD)
    d_probs = jnp.einsum('bqhe,bkhe->bhqk', d_att.astype(f32), values.astype(f32))
    d_scores = (probs * (d_probs - lax.optimization_barrier(jnp.sum(d_probs * probs, axis=-1, keepdims=True))) * hscale).astype(bf16)
    d_query = jnp.einsum('bhqk,bkhe->bqhe', d_scores.astype(f32), keys.astype(f32))
    d_keys = jnp.einsum('bhqk,bqhe->bkhe', d_scores.astype(f32), query.astype(f32))
    d_values = jnp.einsum('bhqk,bqhe->bkhe', probs_b.astype(f32), d_att.astype(f32))
    d_qkv = jnp.concatenate([d_query.reshape(IMG, SEQ, D), d_keys.reshape(IMG, SEQ, D), d_values.reshape(IMG, SEQ, D)], axis=-1).astype(bf16)
    grad_qkv = jnp.einsum('btd,bte->de', normed.astype(f32), d_qkv.astype(f32)) * scale
    return (grad_qkv, grad_proj)

def average(weights, grads):
    f32 = jnp.float32
    total = weights.astype(f32)
    total = total + jnp.roll(weights, 1, axis=0).astype(f32) + jnp.roll(weights, -1, axis=0).astype(f32)
    total = total + jnp.roll(weights, 1, axis=1).astype(f32) + jnp.roll(weights, -1, axis=1).astype(f32)
    return (total / 5.0 - LR * grads).astype(jnp.bfloat16)

def reference(block_input, out_cotangent, w_qkv, w_proj):
    count = N_RX * N_RY
    packed = (block_input.reshape(count, IMG, SEQ, D), out_cotangent.reshape(count, IMG, SEQ, D), w_qkv.reshape(count, D, 3 * D), w_proj.reshape(count, D, D))
    grad_qkv, grad_proj = lax.map(replica_grads, packed)
    grad_qkv = grad_qkv.reshape(N_RX, N_RY, D, 3 * D)
    grad_proj = grad_proj.reshape(N_RX, N_RY, D, D)
    return (average(w_qkv, grad_qkv), average(w_proj, grad_proj))
```

```python
import functools

import jax
import jax.numpy as jnp
from jax import lax
from jax.experimental import pallas as pl
from jax.experimental.pallas import tpu as pltpu
from jax.sharding import PartitionSpec as P

HEADS = 12
LR = 1
F32 = jnp.float32
BF16 = jnp.bfloat16
VMEM_LIMIT = 56 * 2**20


def mm(a,b,ca,cb):
    return lax.dot_general(a,b,(((ca,),(cb,)),((),())),preferred_element_type=F32)

def grads_body(length, heads, tok, cot, wq, wp, gq, gp, normed, qkv, datt, att, dqkv):
    T, D = normed.shape
    hd = D // heads
    scale = D ** -0.5
    hscale = hd ** -0.5
    x = tok[0].astype(F32)
    mean = jnp.mean(x, axis=-1, keepdims=True)
    xc = x - mean
    var = jnp.mean(xc * xc, axis=-1, keepdims=True)
    normed[...] = (xc * lax.rsqrt(var + 1e-06)).astype(BF16)
    for c in range(3):
        cols = slice(c * D, (c + 1) * D)
        qkv[:, cols] = (mm(normed[...], wq[:, cols], 1, 0) * scale).astype(BF16)
    datt[...] = (mm(cot[0], wp[...], 1, 1) * scale).astype(BF16)
    keep = lax.broadcasted_iota(jnp.int32, (T, T), 1) < length
    pack = 128 // hd
    def group(g, _):
        at = [pl.ds(pl.multiple_of(c * D + g * 128, 128), 128) for c in range(3)]
        qg, kg, vg = (qkv[:, a] for a in at)
        dg = datt[:, at[0]]
        outs = [[], [], [], []]
        for j in range(pack):
            s_ = slice(j * hd, (j + 1) * hd)
            q, k, v, da = qg[:, s_], kg[:, s_], vg[:, s_], dg[:, s_]
            s = jnp.where(keep, mm(q, k, 1, 1) * hscale, -1e30)
            e = jnp.exp(s - jnp.max(s, axis=-1, keepdims=True))
            p = e * (1.0 / jnp.sum(e, axis=-1, keepdims=True))
            pb = p.astype(BF16)
            dp = mm(da, v, 1, 1)
            ds = (p * (dp - jnp.sum(dp * p, axis=-1, keepdims=True)) * hscale).astype(BF16)
            outs[0].append(mm(pb, v, 1, 0).astype(BF16))
            outs[1].append(mm(ds, k, 1, 0).astype(BF16))
            outs[2].append(mm(ds, q, 0, 0).astype(BF16))
            outs[3].append(mm(pb, da, 0, 0).astype(BF16))
        o = [jnp.concatenate(z, axis=1) for z in outs]
        att[:, at[0]] = o[0]
        for c in range(3):
            dqkv[:, at[c]] = o[1 + c]
        return 0
    lax.fori_loop(0, heads // pack, group, 0)
    first = pl.program_id(0) == 0
    @pl.when(first)
    def _():
        gq[...] = jnp.zeros_like(gq)
        gp[...] = jnp.zeros_like(gp)
    nt = normed[...].T
    for c in range(3):
        cols = slice(c * D, (c + 1) * D)
        gq[:, cols] += mm(nt, dqkv[:, cols], 1, 0) * scale
    gp[...] += mm(att[...].T, cot[0], 1, 0) * scale

def grads(tokens, cot, wq, wp, heads):
    images, length, D = tokens.shape
    T = -(-length // 16) * 16
    pad = ((0, 0), (0, T - length), (0, 0))
    tokens, cot = jnp.pad(tokens, pad), jnp.pad(cot, pad)
    row = pl.BlockSpec((1, T, D), lambda b: (b, 0, 0))
    full = lambda r, c: pl.BlockSpec((r, c), lambda b: (0, 0))
    return pl.pallas_call(
        functools.partial(grads_body, length, heads),
        grid=(images,),
        in_specs=[row, row, full(D, 3 * D), full(D, D)],
        out_specs=[full(D, 3 * D), full(D, D)],
        out_shape=[jax.ShapeDtypeStruct((D, 3 * D), F32), jax.ShapeDtypeStruct((D, D), F32)],
        scratch_shapes=[pltpu.VMEM((T, D), BF16), pltpu.VMEM((T, 3*D), BF16), pltpu.VMEM((T, D), BF16), pltpu.VMEM((T, D), BF16), pltpu.VMEM((T, 3*D), BF16)],
        compiler_params=pltpu.CompilerParams(vmem_limit_bytes=56 * 2**20, dimension_semantics=("arbitrary",)),
        cost_estimate=pl.CostEstimate(flops=int(9e9), bytes_accessed=int(2e7), transcendentals=int(2e6)),
        name="attention_grads",
    )(tokens, cot, wq, wp)


def permute(block, axis, partner):
    n = lax.axis_size(axis)
    return lax.ppermute(block, axis, [(i, partner(i, n)) for i in range(n)])


def up(i, n):
    return (i + 1) % n


def down(i, n):
    return (i - 1) % n


def near(i, n):
    return i ^ 1


def far(i, n):
    return (i + 1) % n if i % 2 else (i - 1) % n


def opposite(i, n):
    return i ^ 2


def pair_body(wq, bq, wp, bp, after, out):
    rows = wq.shape[0]
    out[:rows] = (wq[...].astype(F32) + bq[...].astype(F32)).astype(BF16)
    width = wp.shape[1]
    for c in range(wp.shape[0] // rows):
        part = slice(c * rows, (c + 1) * rows)
        out[rows:, c * width : (c + 1) * width] = (
            wp[part].astype(F32) + bp[part].astype(F32)
        ).astype(BF16)


def pair_sums(wq, bq, wp, bp, after):
    rows, cols = bq.shape
    last = wq.shape[0] // rows - 1
    return pl.pallas_call(
        pair_body,
        grid=(1,),
        in_specs=[
            pl.BlockSpec((rows, cols), lambda i: (last, 0)),
            pl.BlockSpec(bq.shape, lambda i: (0, 0)),
            pl.BlockSpec(wp.shape, lambda i: (0, 0)),
            pl.BlockSpec(bp.shape, lambda i: (0, 0)),
            pl.BlockSpec(memory_space=pl.ANY),
        ],
        out_specs=pl.BlockSpec((2 * rows, cols), lambda i: (0, 0)),
        out_shape=jax.ShapeDtypeStruct((2 * rows, cols), BF16),
        compiler_params=pltpu.CompilerParams(vmem_limit_bytes=VMEM_LIMIT),
        cost_estimate=pl.CostEstimate(flops=2 * rows * cols, bytes_accessed=12 * rows * cols, transcendentals=0),
        name="pair_sums",
    )(wq, bq, wp, bp, after)


def partial_body(top, gq, wq, nq, fq, aq, gp, wp, np_, acc_q, acc_p):
    i = pl.program_id(0)
    total = wq[...].astype(F32) + nq[...].astype(F32) + fq[...].astype(F32)
    total = total + jnp.where(i < top, aq[...].astype(F32), 0.0)
    acc_q[...] = total / 5.0 - LR * gq[...]
    acc_p[...] = (wp[...].astype(F32) + np_[...].astype(F32)) / 5.0 - LR * gp[...]


def partial_totals(gq, wq, nq, fq, aq, gp, wp, np_):
    block = 128
    steps = wq.shape[0] // block
    top = aq.shape[0] // block
    q = pl.BlockSpec((block, wq.shape[1]), lambda i: (i, 0))
    p = pl.BlockSpec((block, wp.shape[1]), lambda i: (i, 0))
    a = pl.BlockSpec((block, wq.shape[1]), lambda i: (jnp.minimum(i, top - 1), 0))
    return pl.pallas_call(
        functools.partial(partial_body, top),
        grid=(steps,),
        in_specs=[q, q, q, q, a, p, p, p],
        out_specs=[q, p],
        out_shape=[jax.ShapeDtypeStruct(wq.shape, F32), jax.ShapeDtypeStruct(wp.shape, F32)],
        compiler_params=pltpu.CompilerParams(vmem_limit_bytes=VMEM_LIMIT),
        cost_estimate=pl.CostEstimate(flops=10 * wq.size, bytes_accessed=20 * wq.size, transcendentals=0),
        name="partial_totals",
    )(gq, wq, nq, fq, aq, gp, wp, np_)


def final_body(top, acc_q, a2, sq, acc_p, fp, sp, out_q, out_p):
    i = pl.program_id(0)
    late = jnp.where(i < top, a2[...], sq[...]).astype(F32)
    out_q[...] = (acc_q[...] + late / 5.0).astype(BF16)
    out_p[...] = (acc_p[...] + (fp[...].astype(F32) + sp[...].astype(F32)) / 5.0).astype(BF16)


def final_totals(acc_q, a2, acc_p, fp, sums):
    block = 128
    steps = acc_q.shape[0] // block
    top = a2.shape[0] // block
    side = (acc_q.shape[0] - a2.shape[0]) // block
    wide, width = acc_q.shape[1], acc_p.shape[1]
    q = pl.BlockSpec((block, wide), lambda i: (i, 0))
    p = pl.BlockSpec((block, width), lambda i: (i, 0))
    return pl.pallas_call(
        functools.partial(final_body, top),
        grid=(steps,),
        in_specs=[
            q,
            pl.BlockSpec((block, wide), lambda i: (jnp.minimum(i, top - 1), 0)),
            pl.BlockSpec((block, wide), lambda i: (jnp.maximum(i - top, 0), 0)),
            p,
            p,
            pl.BlockSpec((block, width), lambda i: (side + i % side, i // side)),
        ],
        out_specs=[q, p],
        out_shape=[jax.ShapeDtypeStruct(acc_q.shape, BF16), jax.ShapeDtypeStruct(acc_p.shape, BF16)],
        compiler_params=pltpu.CompilerParams(vmem_limit_bytes=VMEM_LIMIT),
        cost_estimate=pl.CostEstimate(flops=4 * acc_q.size, bytes_accessed=10 * acc_q.size, transcendentals=0),
        name="final_totals",
    )(acc_q, a2, sums, acc_p, fp, sums)


def plain_average(weights, grad):
    total = weights.astype(F32)
    for axis in ("rx", "ry"):
        for partner in (up, down):
            total = total + permute(weights, axis, partner).astype(F32)
    return (total / 5.0 - LR * grad).astype(BF16)


def local(block_input, out_cotangent, w_qkv, w_proj):
    wq, wp = w_qkv[0, 0], w_proj[0, 0]
    tokens, cot = block_input[0, 0], out_cotangent[0, 0]
    if lax.axis_size("rx") != 4 or lax.axis_size("ry") % 2:
        gq, gp = grads(tokens, cot, wq, wp, HEADS)
        return plain_average(wq, gq)[None, None], plain_average(wp, gp)[None, None]
    half = wq.shape[0] * 2 // 3
    b1p = permute(wp, "rx", opposite)
    fq = permute(wq, "ry", far)
    a1 = permute(wq[:half], "rx", near)
    b1q = permute(wq[half:], "rx", opposite)
    nq = permute(wq, "ry", near)
    gq, gp = grads(tokens, cot, wq, wp, HEADS)
    a2 = permute(a1, "rx", opposite)
    sums = permute(pair_sums(wq, b1q, wp, b1p, gp), "rx", near)
    fp = permute(wp, "ry", far)
    np_ = permute(wp, "ry", near)
    acc_q, acc_p = partial_totals(gq, wq, nq, fq, a1, gp, wp, np_)
    new_q, new_p = final_totals(acc_q, a2, acc_p, fp, sums)
    return new_q[None, None], new_p[None, None]


def solution(mesh):
    return jax.shard_map(
        local,
        mesh=mesh,
        in_specs=(
            P("rx", "ry", None, None, None),
            P("rx", "ry", None, None, None),
            P("rx", "ry", None, None),
            P("rx", "ry", None, None),
        ),
        out_specs=(P("rx", "ry", None, None), P("rx", "ry", None, None)),
        check_vma=False,
    )
```

```python
import functools

import jax
import jax.numpy as jnp
from jax import lax
from jax.experimental import pallas as pl
from jax.experimental.pallas import tpu as pltpu
from jax.sharding import PartitionSpec as P

HEADS = 12
LR = 1
F32 = jnp.float32
BF16 = jnp.bfloat16
MIB = 2**20


def mm(a, b, ca, cb):
    return lax.dot_general(a, b, (((ca,), (cb,)), ((), ())), preferred_element_type=F32)


def call(body, outs, operands, name, flops, moved, vmem, grid=None, in_specs=None, out_specs=None, scratch=(), exps=0):
    whole = pl.BlockSpec(memory_space=pltpu.VMEM)
    kwargs = {} if grid is None else {"grid": grid}
    return pl.pallas_call(
        body,
        in_specs=in_specs or [whole] * len(operands),
        out_specs=out_specs or [whole] * len(outs),
        out_shape=[jax.ShapeDtypeStruct(shape, dtype) for shape, dtype in outs],
        scratch_shapes=list(scratch),
        compiler_params=pltpu.CompilerParams(vmem_limit_bytes=vmem * MIB),
        cost_estimate=pl.CostEstimate(flops=flops, bytes_accessed=moved, transcendentals=exps),
        name=name,
        **kwargs,
    )(*operands)


def project_body(rows, tok, cot, wq, wp, turned, qkv, datt, normed):
    c = pl.program_id(0)
    total, width = normed.shape
    scale = width**-0.5

    @pl.when(c == 0)
    def _():
        for r in range(0, total, rows):
            part = slice(r, r + rows)
            x = tok[part].astype(F32)
            xc = x - jnp.mean(x, axis=-1, keepdims=True)
            var = jnp.mean(xc * xc, axis=-1, keepdims=True)
            normed[part] = (xc * lax.rsqrt(var + 1e-06)).astype(BF16)
            datt[part] = (mm(cot[part], wp[...], 1, 1) * scale).astype(BF16)
        turned[...] = normed[...].T

    for r in range(0, total, rows):
        part = slice(r, r + rows)
        qkv[part] = (mm(normed[part], wq[...], 1, 0) * scale).astype(BF16)


def project(tokens, cot, wq, wp, rows):
    total, width = tokens.shape
    fixed = pl.BlockSpec((total, width), lambda c: (0, 0))
    return call(
        functools.partial(project_body, rows),
        [((width, total), BF16), ((total, 3 * width), BF16), ((total, width), BF16)],
        (tokens, cot, wq, wp),
        "project",
        flops=8 * total * width * width,
        moved=16 * total * width + 8 * width * width,
        vmem=32,
        grid=(3,),
        in_specs=[
            fixed,
            fixed,
            pl.BlockSpec((width, width), lambda c: (0, c)),
            pl.BlockSpec((width, width), lambda c: (0, 0)),
        ],
        out_specs=[
            pl.BlockSpec((width, total), lambda c: (0, 0)),
            pl.BlockSpec((total, width), lambda c: (0, c)),
            fixed,
        ],
        scratch=[pltpu.VMEM((total, width), BF16)],
    )


def attention_body(length, heads, unroll, qkv, datt, att, dqkv):
    rows, width = datt.shape
    hd = width // heads
    hscale = hd**-0.5
    pack = 128 // hd
    full = rows // 16 * 16 - 16
    keep = lax.broadcasted_iota(jnp.int32, (rows - full, rows), 0) < length - full
    lane = lax.broadcasted_iota(jnp.int32, (rows, 128), 1)

    def group(g, carry):
        at = [pl.ds(pl.multiple_of(c * width + g * 128, 128), 128) for c in range(3)]
        qg, kg, vg = (qkv[:, a] for a in at)
        dg = datt[:, at[0]]
        kt, vt = kg.T, vg.T
        dk, dv, at_t, dq_t = 0.0, 0.0, [], []
        for j in range(pack):
            own = (lane >= j * hd) & (lane < (j + 1) * hd)
            q = jnp.where(own, qg, jnp.zeros_like(qg)) * jnp.asarray(hscale, BF16)
            da = jnp.where(own, dg, jnp.zeros_like(dg))
            s = mm(kg, q, 1, 1)
            s = jnp.concatenate([s[:full], jnp.where(keep, s[full:], -1e30)], axis=0)
            e = jnp.exp(s - jnp.max(s, axis=0, keepdims=True))
            p = e * (1.0 / jnp.sum(e, axis=0, keepdims=True))
            pb = p.astype(BF16)
            dp = mm(vg, da, 1, 1)
            ds = (p * (dp - jnp.sum(dp * p, axis=0, keepdims=True))).astype(BF16)
            mine = slice(j * hd, (j + 1) * hd)
            at_t.append(mm(vt[mine], pb, 1, 0))
            dq_t.append(mm(kt[mine], ds, 1, 0) * hscale)
            dk = dk + mm(ds, q, 1, 0)
            dv = dv + mm(pb, da, 1, 0)
        att[pl.ds(pl.multiple_of(g * 128, 128), 128), :] = jnp.concatenate(at_t, axis=0).astype(BF16)
        dqkv[:, at[0]] = jnp.concatenate(dq_t, axis=0).astype(BF16).T
        dqkv[:, at[1]] = dk.astype(BF16)
        dqkv[:, at[2]] = dv.astype(BF16)
        return carry

    lax.fori_loop(0, heads // pack, group, 0, unroll=unroll)


def attention(qkv, datt, first, count, rows, length, heads, unroll=6):
    width = datt.shape[1]
    here = lambda b: (b + first, 0)
    there = lambda b: (b, 0)
    return call(
        functools.partial(attention_body, length, heads, unroll),
        [((count * width, rows), BF16), ((count * rows, 3 * width), BF16)],
        (qkv, datt),
        "attention",
        flops=12 * count * rows * 256 * 256 * heads,
        moved=16 * count * rows * width,
        vmem=16,
        grid=(count,),
        in_specs=[pl.BlockSpec((rows, 3 * width), here), pl.BlockSpec((rows, width), here)],
        out_specs=[pl.BlockSpec((width, rows), there), pl.BlockSpec((rows, 3 * width), there)],
        exps=count * heads * rows * rows,
    )


def weight_grad(left, rights):
    at, total = 0, 0.0
    for right in rights:
        total = total + mm(left[:, at : at + right.shape[0]], right[...], 1, 0)
        at += right.shape[0]
    return total


def partial_body(top, parts, normed, wq, nq, a1, *refs):
    dqkv, acc = refs[:parts], refs[parts]
    i = pl.program_id(0)
    scale = (wq.shape[1] // 3) ** -0.5
    total = wq[...].astype(F32) + nq[...].astype(F32)
    total = total + jnp.where(i < top, a1[...].astype(F32), 0.0)
    acc[...] = total / 5.0 - LR * (weight_grad(normed, dqkv) * scale)


def partial_qkv(normed, dqkv, wq, nq, a1, block):
    width, total = normed.shape
    wide = wq.shape[1]
    top = a1.shape[0] // block
    row = pl.BlockSpec((block, wide), lambda i: (i, 0))
    return call(
        functools.partial(partial_body, top, len(dqkv)),
        [(wq.shape, F32)],
        (normed, wq, nq, a1, *dqkv),
        "partial_qkv",
        flops=2 * total * width * wide,
        moved=12 * width * wide,
        vmem=32,
        grid=(width // block,),
        in_specs=[
            pl.BlockSpec((block, total), lambda i: (i, 0)),
            row,
            row,
            pl.BlockSpec((block, wide), lambda i: (jnp.minimum(i, top - 1), 0)),
            *[pl.BlockSpec(d.shape, lambda i: (0, 0)) for d in dqkv],
        ],
        out_specs=[row],
    )[0]


def proj_body(parts, cot, wp, np_, fp, sp, *refs):
    att, out = refs[:parts], refs[parts]
    scale = wp.shape[0] ** -0.5
    total = wp[...].astype(F32) + np_[...].astype(F32) + fp[...].astype(F32) + sp[...].astype(F32)
    rows, width = att[0].shape[1], wp.shape[1]
    at, grad = 0, 0.0
    for a in att:
        for r in range(0, a.shape[0], width):
            grad = grad + mm(a[r : r + width], cot[at : at + rows], 1, 0)
            at += rows
    out[...] = (total / 5.0 - LR * (grad * scale)).astype(BF16)


def new_proj(cot, att, wp, np_, fp, sp):
    total, width = cot.shape
    return call(
        functools.partial(proj_body, len(att)),
        [(wp.shape, BF16)],
        (cot, wp, np_, fp, sp, *att),
        "new_proj",
        flops=2 * total * width * width,
        moved=12 * width * width,
        vmem=16,
    )[0]


def final_body(top, side, acc, fq, a2, s2, other, out):
    i = pl.program_id(0)
    half = (pl.num_programs(0) - top) // 2
    mine = (i - top) // half == side[0]
    rest = jnp.where(mine, s2[...], other[...])
    late = fq[...].astype(F32) + jnp.where(i < top, a2[...], rest).astype(F32)
    out[...] = (acc[...] + late / 5.0).astype(BF16)


def final_qkv(side, acc, fq, a2, s2, other, block):
    rows, wide = acc.shape
    top, half = a2.shape[0] // block, s2.shape[0] // block
    row = lambda at: pl.BlockSpec((block, wide), lambda i: (at(i), 0))
    low = row(lambda i: jnp.maximum(i - top, 0) % half)
    return call(
        functools.partial(final_body, top),
        [(acc.shape, BF16)],
        (side, acc, fq, a2, s2, other),
        "final_qkv",
        flops=4 * rows * wide,
        moved=10 * rows * wide,
        vmem=16,
        grid=(rows // block,),
        in_specs=[
            pl.BlockSpec(memory_space=pltpu.SMEM),
            row(lambda i: i),
            row(lambda i: i),
            row(lambda i: jnp.minimum(i, top - 1)),
            low,
            low,
        ],
        out_specs=[row(lambda i: i)],
    )[0]


def pair_body(a, b, out):
    out[...] = (a[...].astype(F32) + b[...].astype(F32)).astype(BF16)


def pair_sum(a, b):
    return call(
        pair_body, [(a.shape, BF16)], (a, b), "pair_sum", flops=a.size, moved=6 * a.size, vmem=8
    )[0]


def rows_body(count, source, out, done):
    copy = pltpu.make_async_copy(source.at[:count], out, done)
    copy.start()
    copy.wait()


def first_rows(a, count):
    return call(
        functools.partial(rows_body, count),
        [((count, a.shape[1]), a.dtype)],
        (a,),
        "first_rows",
        flops=0,
        moved=4 * count * a.shape[1],
        vmem=8,
        in_specs=[pl.BlockSpec(memory_space=pl.ANY)],
        scratch=[pltpu.SemaphoreType.DMA],
    )[0]


def permute(block, axis, partner):
    n = lax.axis_size(axis)
    return lax.ppermute(block, axis, [(i, partner(i, n)) for i in range(n)])


def up(i, n):
    return (i + 1) % n


def down(i, n):
    return (i - 1) % n


def near(i, n):
    return i ^ 1


def far(i, n):
    return (i + 1) % n if i % 2 else (i - 1) % n


def opposite(i, n):
    return i ^ 2


def after(values, *others):
    return lax.optimization_barrier((values, others))[0]


def plain_average(weights, grad):
    total = weights.astype(F32)
    for axis in ("rx", "ry"):
        for partner in (up, down):
            total = total + permute(weights, axis, partner).astype(F32)
    return (total / 5.0 - LR * grad).astype(BF16)


def local(block_input, out_cotangent, w_qkv, w_proj):
    wq, wp = w_qkv[0, 0], w_proj[0, 0]
    images, length, width = block_input.shape[2:]
    rows = -(-length // 16) * 16
    pad = ((0, 0), (0, rows - length), (0, 0))
    tokens = jnp.pad(block_input[0, 0], pad).reshape(images * rows, width)
    cot = jnp.pad(out_cotangent[0, 0], pad).reshape(images * rows, width)
    half = images // 2

    if lax.axis_size("rx") != 4 or lax.axis_size("ry") % 2:
        normed, qkv, datt = project(tokens, cot, wq, wp, rows)
        att, dqkv = attention(qkv, datt, 0, images, rows, length, HEADS)
        scale = width**-0.5
        gq = mm(normed, dqkv, 1, 0) * scale
        gp = jnp.einsum("bdt,bte->de", att.reshape(images, width, rows), cot.reshape(images, rows, width), preferred_element_type=F32) * scale
        return plain_average(wq, gq)[None, None], plain_average(wp, gp)[None, None]

    block = width // 8
    cut, part = 4 * block, 2 * block
    side = lax.axis_index("rx") // 2
    top = first_rows(wq, cut)
    sent = lax.dynamic_slice_in_dim(wq, cut + (1 - side) * part, part)
    kept = lax.dynamic_slice_in_dim(wq, cut + side * part, part)
    b1 = permute(wp, "rx", opposite)
    fp = permute(wp, "ry", far)
    a1 = permute(top, "rx", near)
    nq = permute(wq, "ry", near)
    np_ = permute(wp, "ry", near)
    normed, qkv, datt = project(tokens, cot, wq, wp, rows)

    wq2, sent, qkv, datt = after((wq, sent, qkv, datt), nq, np_)
    b2 = permute(sent, "rx", opposite)
    fq = permute(wq2, "ry", far)
    att0, dqkv0 = attention(qkv, datt, 0, half, rows, length, HEADS)

    b1, fp = after((b1, fp), att0)
    qkv, datt = after((qkv, datt), b1, fp)
    att1, dqkv1 = attention(qkv, datt, half, images - half, rows, length, HEADS)

    a1, b2 = after((a1, b2), att1)
    a2 = permute(a1, "rx", opposite)
    pair2 = pair_sum(kept, b2)
    s2 = permute(pair2, "rx", near)
    dqkv0, dqkv1 = after((dqkv0, dqkv1), pair2)
    acc = partial_qkv(normed, (dqkv0, dqkv1), wq, nq, a1, block)
    s2 = after(s2, acc)
    other = permute(s2, "rx", opposite)
    pair1 = pair_sum(wp, after(b1, s2))
    s1 = permute(pair1, "rx", near)
    out_p = new_proj(cot, (att0, att1), wp, np_, fp, s1)
    out_q = final_qkv(side.reshape(1), acc, fq, a2, s2, other, block)
    return out_q[None, None], out_p[None, None]


def solution(mesh):
    return jax.shard_map(
        local,
        mesh=mesh,
        in_specs=(
            P("rx", "ry", None, None, None),
            P("rx", "ry", None, None, None),
            P("rx", "ry", None, None),
            P("rx", "ry", None, None),
        ),
        out_specs=(P("rx", "ry", None, None), P("rx", "ry", None, None)),
        check_vma=False,
    )
```

```python
import functools

import jax
import jax.numpy as jnp
from jax import lax
from jax.experimental import pallas as pl
from jax.experimental.pallas import tpu as pltpu
from jax.sharding import PartitionSpec as P

HEADS = 12
LR = 1
F32 = jnp.float32
BF16 = jnp.bfloat16
MIB = 2**20


def mm(a, b, ca, cb):
    return lax.dot_general(a, b, (((ca,), (cb,)), ((), ())), preferred_element_type=F32)


def call(body, outs, operands, name, flops, moved, vmem, grid=None, in_specs=None, out_specs=None, scratch=(), exps=0, aliases=None, hint=1):
    whole = pl.BlockSpec(memory_space=pltpu.VMEM)
    kwargs = {} if grid is None else {"grid": grid}
    return pl.pallas_call(
        body,
        in_specs=in_specs or [whole] * len(operands),
        out_specs=out_specs or [whole] * len(outs),
        out_shape=[jax.ShapeDtypeStruct(shape, dtype) for shape, dtype in outs],
        scratch_shapes=list(scratch),
        compiler_params=pltpu.CompilerParams(vmem_limit_bytes=vmem * MIB),
        cost_estimate=pl.CostEstimate(flops=int(flops * hint), bytes_accessed=int(moved * hint), transcendentals=int(exps * hint)),
        input_output_aliases=aliases or {},
        name=name,
        **kwargs,
    )(*operands)


def project_body(rows, tok, cot, wq, wp, turned, qkv, datt, normed):
    c = pl.program_id(0)
    total, width = normed.shape
    scale = width**-0.5

    @pl.when(c == 0)
    def _():
        for r in range(0, total, rows):
            part = slice(r, r + rows)
            x = tok[part].astype(F32)
            xc = x - jnp.mean(x, axis=-1, keepdims=True)
            var = jnp.mean(xc * xc, axis=-1, keepdims=True)
            normed[part] = (xc * lax.rsqrt(var + 1e-06)).astype(BF16)
            datt[part] = (mm(cot[part], wp[...], 1, 1) * scale).astype(BF16)
        turned[...] = normed[...].T

    for r in range(0, total, rows):
        part = slice(r, r + rows)
        qkv[part] = (mm(normed[part], wq[...], 1, 0) * scale).astype(BF16)


def project(tokens, cot, wq, wp, rows):
    total, width = tokens.shape
    fixed = pl.BlockSpec((total, width), lambda c: (0, 0))
    return call(
        functools.partial(project_body, rows),
        [((width, total), BF16), ((total, 3 * width), BF16), ((total, width), BF16)],
        (tokens, cot, wq, wp),
        "project",
        flops=8 * total * width * width,
        moved=16 * total * width + 8 * width * width,
        vmem=32,
        grid=(3,),
        in_specs=[
            fixed,
            fixed,
            pl.BlockSpec((width, width), lambda c: (0, c)),
            pl.BlockSpec((width, width), lambda c: (0, 0)),
        ],
        out_specs=[
            pl.BlockSpec((width, total), lambda c: (0, 0)),
            pl.BlockSpec((total, width), lambda c: (0, c)),
            fixed,
        ],
        scratch=[pltpu.VMEM((total, width), BF16)],
    )


def attention_body(length, heads, unroll, qkv, datt, att, dqkv):
    rows, width = datt.shape
    hd = width // heads
    hscale = hd**-0.5
    pack = 128 // hd
    full = rows // 16 * 16 - 16
    keep = lax.broadcasted_iota(jnp.int32, (rows - full, rows), 0) < length - full
    lane = lax.broadcasted_iota(jnp.int32, (rows, 128), 1)

    def group(g, carry):
        at = [pl.ds(pl.multiple_of(c * width + g * 128, 128), 128) for c in range(3)]
        qg, kg, vg = (qkv[:, a] for a in at)
        dg = datt[:, at[0]]
        kt, vt = kg.T, vg.T
        dk, dv, at_t, dq_t = 0.0, 0.0, [], []
        for j in range(pack):
            own = (lane >= j * hd) & (lane < (j + 1) * hd)
            q = jnp.where(own, qg, jnp.zeros_like(qg)) * jnp.asarray(hscale, BF16)
            da = jnp.where(own, dg, jnp.zeros_like(dg))
            s = mm(kg, q, 1, 1)
            s = jnp.concatenate([s[:full], jnp.where(keep, s[full:], -1e30)], axis=0)
            e = jnp.exp(s - jnp.max(s, axis=0, keepdims=True))
            p = e * (1.0 / jnp.sum(e, axis=0, keepdims=True))
            pb = p.astype(BF16)
            dp = mm(vg, da, 1, 1)
            ds = (p * (dp - jnp.sum(dp * p, axis=0, keepdims=True))).astype(BF16)
            mine = slice(j * hd, (j + 1) * hd)
            at_t.append(mm(vt[mine], pb, 1, 0))
            dq_t.append(mm(kt[mine], ds, 1, 0) * hscale)
            dk = dk + mm(ds, q, 1, 0)
            dv = dv + mm(pb, da, 1, 0)
        att[pl.ds(pl.multiple_of(g * 128, 128), 128), :] = jnp.concatenate(at_t, axis=0).astype(BF16)
        dqkv[:, at[0]] = jnp.concatenate(dq_t, axis=0).astype(BF16).T
        dqkv[:, at[1]] = dk.astype(BF16)
        dqkv[:, at[2]] = dv.astype(BF16)
        return carry

    lax.fori_loop(0, heads // pack, group, 0, unroll=unroll)


def attention(qkv, datt, first, count, rows, length, heads, hint=1, unroll=6):
    width = datt.shape[1]
    here = lambda b: (b + first, 0)
    there = lambda b: (b, 0)
    return call(
        functools.partial(attention_body, length, heads, unroll),
        [((count * width, rows), BF16), ((count * rows, 3 * width), BF16)],
        (qkv, datt),
        "attention",
        flops=12 * count * rows * 256 * 256 * heads,
        moved=16 * count * rows * width,
        vmem=16,
        grid=(count,),
        in_specs=[pl.BlockSpec((rows, 3 * width), here), pl.BlockSpec((rows, width), here)],
        out_specs=[pl.BlockSpec((width, rows), there), pl.BlockSpec((rows, 3 * width), there)],
        exps=count * heads * rows * rows,
        hint=hint,
    )


def partial_body(parts, normed, wq, nq, a1, *refs):
    dqkv, acc = refs[:parts], refs[parts]
    rows, wide = wq.shape
    width = wide // 3
    scale = width**-0.5
    for first, last in ((0, a1.shape[0]), (a1.shape[0], rows)):
        part = slice(first, last)
        for c in range(0, wide, width):
            cols = slice(c, c + width)
            at, grad = 0, 0.0
            for d in dqkv:
                grad = grad + mm(normed[part, at : at + d.shape[0]], d[:, cols], 1, 0)
                at += d.shape[0]
            total = wq[part, cols].astype(F32) + nq[part, cols].astype(F32)
            if first == 0:
                total = total + a1[:, cols].astype(F32)
            acc[part, cols] = total * 0.2 - LR * (grad * scale)


def partial_qkv(normed, dqkv, wq, nq, a1):
    width, total = normed.shape
    wide = wq.shape[1]
    return call(
        functools.partial(partial_body, len(dqkv)),
        [(wq.shape, F32)],
        (normed, wq, nq, a1, *dqkv),
        "partial_qkv",
        flops=2 * total * width * wide,
        moved=12 * width * wide,
        vmem=16,
    )[0]


def partial_proj_body(parts, cot, wp, np_, fp, *refs):
    att, acc = refs[:parts], refs[parts]
    scale = wp.shape[0] ** -0.5
    total = wp[...].astype(F32) + np_[...].astype(F32) + fp[...].astype(F32)
    rows, width = att[0].shape[1], wp.shape[1]
    at, grad = 0, 0.0
    for a in att:
        for r in range(0, a.shape[0], width):
            grad = grad + mm(a[r : r + width], cot[at : at + rows], 1, 0)
            at += rows
    acc[...] = total * 0.2 - LR * (grad * scale)


def partial_proj(cot, att, wp, np_, fp):
    total, width = cot.shape
    return call(
        functools.partial(partial_proj_body, len(att)),
        [(wp.shape, F32)],
        (cot, wp, np_, fp, *att),
        "partial_proj",
        flops=2 * total * width * width,
        moved=12 * width * width,
        vmem=16,
        hint=10,
    )[0]


def final_proj_body(acc, s1, out):
    out[...] = (acc[...] + s1[...].astype(F32) * 0.2).astype(BF16)


def final_proj(acc, s1):
    return call(
        final_proj_body,
        [(acc.shape, BF16)],
        (acc, s1),
        "final_proj",
        flops=2 * acc.size,
        moved=8 * acc.size,
        vmem=8,
    )[0]


def final_body(cuts, side, acc, fq, a2, s2, other, out, held, done):
    top, half = a2.shape[0], s2.shape[0]
    copies = []
    for k, (first, last) in enumerate(zip(cuts, cuts[1:])):
        part = slice(first, last)
        if first < top:
            late = a2[part]
        else:
            low = slice((first - top) % half, (first - top) % half + last - first)
            late = jnp.where(side[0] == (first - top) // half, s2[low], other[low])
        late = fq[part].astype(F32) + late.astype(F32)
        held[part] = (acc[part] + late * 0.2).astype(BF16)
        part = pl.ds(first, last - first)
        copies.append(pltpu.make_async_copy(held.at[part], out.at[part], done.at[k]))
        copies[-1].start()
    for copy in copies:
        copy.wait()


def final_qkv(side, acc, fq, a2, s2, other):
    rows, wide = acc.shape
    top, half = a2.shape[0], s2.shape[0]
    cuts = []
    for first, last in ((0, top), (top, top + half), (top + half, rows)):
        steps = max(1, (last - first) // 96)
        cuts += [first + (last - first) * k // steps // 16 * 16 for k in range(steps)]
    cuts = (*cuts, rows)
    whole = pl.BlockSpec(memory_space=pltpu.VMEM)
    return call(
        functools.partial(final_body, cuts),
        [(acc.shape, BF16)],
        (side, acc, fq, a2, s2, other),
        "final_qkv",
        flops=4 * rows * wide,
        moved=10 * rows * wide,
        vmem=16,
        in_specs=[pl.BlockSpec(memory_space=pltpu.SMEM)] + [whole] * 5,
        out_specs=[pl.BlockSpec(memory_space=pl.ANY)],
        scratch=[pltpu.VMEM((rows, wide), BF16), pltpu.SemaphoreType.DMA((len(cuts) - 1,))],
    )[0]


def pair_body(a, b, out):
    out[...] = (a[...].astype(F32) + b[...].astype(F32)).astype(BF16)


def pair_sum(a, b):
    return call(
        pair_body, [(a.shape, BF16)], (a, b), "pair_sum", flops=a.size, moved=6 * a.size, vmem=8
    )[0]


def rows_body(source, out, done):
    pieces = done.shape[0]
    rows = out.shape[0] // pieces
    copies = []
    for k in range(pieces):
        part = pl.ds(k * rows, rows)
        copies.append(pltpu.make_async_copy(source.at[part], out.at[part], done.at[k]))
    for copy in copies:
        copy.start()
    for copy in copies:
        copy.wait()


def first_rows(a, count):
    return call(
        rows_body,
        [((count, a.shape[1]), a.dtype)],
        (a,),
        "first_rows",
        flops=0,
        moved=4 * count * a.shape[1],
        vmem=8,
        in_specs=[pl.BlockSpec(memory_space=pltpu.HBM)],
        scratch=[pltpu.SemaphoreType.DMA((2,))],
    )[0]


def permute(block, axis, partner):
    n = lax.axis_size(axis)
    return lax.ppermute(block, axis, [(i, partner(i, n)) for i in range(n)])


def up(i, n):
    return (i + 1) % n


def down(i, n):
    return (i - 1) % n


def near(i, n):
    return i ^ 1


def far(i, n):
    return (i + 1) % n if i % 2 else (i - 1) % n


def opposite(i, n):
    return i ^ 2


def after(values, *others):
    return lax.optimization_barrier((values, others))[0]


def plain_average(weights, grad):
    total = weights.astype(F32)
    for axis in ("rx", "ry"):
        for partner in (up, down):
            total = total + permute(weights, axis, partner).astype(F32)
    return (total / 5.0 - LR * grad).astype(BF16)


def local(block_input, out_cotangent, w_qkv, w_proj):
    wq, wp = w_qkv[0, 0], w_proj[0, 0]
    images, length, width = block_input.shape[2:]
    rows = -(-length // 16) * 16
    pad = ((0, 0), (0, rows - length), (0, 0))
    tokens = jnp.pad(block_input[0, 0], pad).reshape(images * rows, width)
    cot = jnp.pad(out_cotangent[0, 0], pad).reshape(images * rows, width)
    half = images // 2

    if lax.axis_size("rx") != 4 or lax.axis_size("ry") % 2:
        normed, qkv, datt = project(tokens, cot, wq, wp, rows)
        att, dqkv = attention(qkv, datt, 0, images, rows, length, HEADS)
        scale = width**-0.5
        gq = mm(normed, dqkv, 1, 0) * scale
        gp = jnp.einsum("bdt,bte->de", att.reshape(images, width, rows), cot.reshape(images, rows, width), preferred_element_type=F32) * scale
        return plain_average(wq, gq)[None, None], plain_average(wp, gp)[None, None]

    cut = width * 11 // 24
    part = (width - cut) // 2
    side = lax.axis_index("rx") // 2
    top = first_rows(wq, cut)
    sent = lax.dynamic_slice_in_dim(wq, cut + (1 - side) * part, part)
    kept = lax.dynamic_slice_in_dim(wq, cut + side * part, part)
    b1 = permute(wp, "rx", opposite)
    fp = permute(wp, "ry", far)
    a1 = permute(top, "rx", near)
    nq = permute(wq, "ry", near)
    np_ = permute(wp, "ry", near)
    normed, qkv, datt = project(tokens, cot, wq, wp, rows)

    wq2, sent, qkv, datt = after((wq, sent, qkv, datt), nq, np_)
    b2 = permute(sent, "rx", opposite)
    fq = permute(wq2, "ry", far)
    att0, dqkv0 = attention(qkv, datt, 0, half, rows, length, HEADS)

    b1, fp = after((b1, fp), att0)
    qkv, datt = after((qkv, datt), b1, fp)
    att1, dqkv1 = attention(qkv, datt, half, images - half, rows, length, HEADS)

    a1, b2 = after(a1, att1), after(b2, att1)
    a2 = permute(a1, "rx", opposite)
    pair2 = pair_sum(kept, b2)
    s2 = permute(pair2, "rx", near)
    dqkv0, dqkv1 = after((dqkv0, dqkv1), pair2)
    acc = partial_qkv(normed, (dqkv0, dqkv1), wq, nq, a1)
    s2 = after(s2, acc)
    other = permute(s2, "rx", opposite)
    pair1 = pair_sum(wp, after(b1, s2))
    s1 = permute(pair1, "rx", near)
    acc_p = partial_proj(cot, after((att0, att1), pair1, a2), wp, np_, fp)
    out_p = final_proj(acc_p, s1)
    fq, a2, other = after((fq, a2, other), out_p)
    out_q = final_qkv(side.reshape(1), acc, fq, a2, s2, other)
    return out_q[None, None], out_p[None, None]


def solution(mesh):
    return jax.shard_map(
        local,
        mesh=mesh,
        in_specs=(
            P("rx", "ry", None, None, None),
            P("rx", "ry", None, None, None),
            P("rx", "ry", None, None),
            P("rx", "ry", None, None),
        ),
        out_specs=(P("rx", "ry", None, None), P("rx", "ry", None, None)),
        check_vma=False,
    )
```

```python
import functools

import jax
import jax.numpy as jnp
from jax import lax
from jax.experimental import pallas as pl
from jax.experimental.pallas import tpu as pltpu
from jax.sharding import PartitionSpec as P

HEADS = 12
LR = 1
F32 = jnp.float32
BF16 = jnp.bfloat16
MIB = 2**20


def mm(a, b, ca, cb):
    return lax.dot_general(a, b, (((ca,), (cb,)), ((), ())), preferred_element_type=F32)


def call(body, outs, operands, name, flops, moved, vmem, grid=None, in_specs=None, out_specs=None, scratch=(), exps=0, aliases=None, hint=1):
    whole = pl.BlockSpec(memory_space=pltpu.VMEM)
    kwargs = {} if grid is None else {"grid": grid}
    return pl.pallas_call(
        body,
        in_specs=in_specs or [whole] * len(operands),
        out_specs=out_specs or [whole] * len(outs),
        out_shape=[jax.ShapeDtypeStruct(shape, dtype) for shape, dtype in outs],
        scratch_shapes=list(scratch),
        compiler_params=pltpu.CompilerParams(vmem_limit_bytes=vmem * MIB),
        cost_estimate=pl.CostEstimate(flops=int(flops * hint), bytes_accessed=int(moved * hint), transcendentals=int(exps * hint)),
        input_output_aliases=aliases or {},
        name=name,
        **kwargs,
    )(*operands)


def project_body(rows, tok, cot, wq, wp, turned, qkv, datt, normed):
    c = pl.program_id(0)
    total, width = normed.shape
    scale = width**-0.5

    @pl.when(c == 0)
    def _():
        for r in range(0, total, rows):
            part = slice(r, r + rows)
            x = tok[part].astype(F32)
            xc = x - jnp.mean(x, axis=-1, keepdims=True)
            var = jnp.mean(xc * xc, axis=-1, keepdims=True)
            normed[part] = (xc * lax.rsqrt(var + 1e-06)).astype(BF16)
            datt[part] = (mm(cot[part], wp[...], 1, 1) * scale).astype(BF16)
        turned[...] = normed[...].T

    for r in range(0, total, rows):
        part = slice(r, r + rows)
        qkv[part] = (mm(normed[part], wq[...], 1, 0) * scale).astype(BF16)


def project(tokens, cot, wq, wp, rows):
    total, width = tokens.shape
    fixed = pl.BlockSpec((total, width), lambda c: (0, 0))
    return call(
        functools.partial(project_body, rows),
        [((width, total), BF16), ((total, 3 * width), BF16), ((total, width), BF16)],
        (tokens, cot, wq, wp),
        "project",
        flops=8 * total * width * width,
        moved=16 * total * width + 8 * width * width,
        vmem=32,
        grid=(3,),
        in_specs=[
            fixed,
            fixed,
            pl.BlockSpec((width, width), lambda c: (0, c)),
            pl.BlockSpec((width, width), lambda c: (0, 0)),
        ],
        out_specs=[
            pl.BlockSpec((width, total), lambda c: (0, 0)),
            pl.BlockSpec((total, width), lambda c: (0, c)),
            fixed,
        ],
        scratch=[pltpu.VMEM((total, width), BF16)],
    )


def attention_body(length, heads, unroll, qkv, datt, att, dqkv):
    rows, width = datt.shape
    hd = width // heads
    hscale = hd**-0.5
    pack = 128 // hd
    full = rows // 16 * 16 - 16
    keep = lax.broadcasted_iota(jnp.int32, (rows - full, rows), 0) < length - full
    lane = lax.broadcasted_iota(jnp.int32, (rows, 128), 1)

    def group(g, carry):
        at = [pl.ds(pl.multiple_of(c * width + g * 128, 128), 128) for c in range(3)]
        qg, kg, vg = (qkv[:, a] for a in at)
        dg = datt[:, at[0]]
        kt, vt = kg.T, vg.T
        dk, dv, at_t, dq_t = 0.0, 0.0, [], []
        for j in range(pack):
            own = (lane >= j * hd) & (lane < (j + 1) * hd)
            q = jnp.where(own, qg, jnp.zeros_like(qg)) * jnp.asarray(hscale, BF16)
            da = jnp.where(own, dg, jnp.zeros_like(dg))
            s = mm(kg, q, 1, 1)
            s = jnp.concatenate([s[:full], jnp.where(keep, s[full:], -1e30)], axis=0)
            e = jnp.exp(s - jnp.max(s, axis=0, keepdims=True))
            p = e * (1.0 / jnp.sum(e, axis=0, keepdims=True))
            pb = p.astype(BF16)
            dp = mm(vg, da, 1, 1)
            ds = (p * (dp - jnp.sum(dp * p, axis=0, keepdims=True))).astype(BF16)
            mine = slice(j * hd, (j + 1) * hd)
            at_t.append(mm(vt[mine], pb, 1, 0))
            dq_t.append(mm(kt[mine], ds, 1, 0) * hscale)
            dk = dk + mm(ds, q, 1, 0)
            dv = dv + mm(pb, da, 1, 0)
        att[pl.ds(pl.multiple_of(g * 128, 128), 128), :] = jnp.concatenate(at_t, axis=0).astype(BF16)
        dqkv[:, at[0]] = jnp.concatenate(dq_t, axis=0).astype(BF16).T
        dqkv[:, at[1]] = dk.astype(BF16)
        dqkv[:, at[2]] = dv.astype(BF16)
        return carry

    lax.fori_loop(0, heads // pack, group, 0, unroll=unroll)


def attention(qkv, datt, first, count, rows, length, heads, hint=1, unroll=6):
    width = datt.shape[1]
    here = lambda b: (b + first, 0)
    there = lambda b: (b, 0)
    return call(
        functools.partial(attention_body, length, heads, unroll),
        [((count * width, rows), BF16), ((count * rows, 3 * width), BF16)],
        (qkv, datt),
        "attention",
        flops=12 * count * rows * 256 * 256 * heads,
        moved=16 * count * rows * width,
        vmem=16,
        grid=(count,),
        in_specs=[pl.BlockSpec((rows, 3 * width), here), pl.BlockSpec((rows, width), here)],
        out_specs=[pl.BlockSpec((width, rows), there), pl.BlockSpec((rows, 3 * width), there)],
        exps=count * heads * rows * rows,
        hint=hint,
    )


def partial_body(parts, normed, wq, nq, a1, *refs):
    dqkv, acc = refs[:parts], refs[parts]
    rows, wide = wq.shape
    width = wide // 3
    scale = width**-0.5
    for first, last in ((0, a1.shape[0]), (a1.shape[0], rows)):
        part = slice(first, last)
        for c in range(0, wide, width):
            cols = slice(c, c + width)
            at, grad = 0, 0.0
            for d in dqkv:
                grad = grad + mm(normed[part, at : at + d.shape[0]], d[:, cols], 1, 0)
                at += d.shape[0]
            total = wq[part, cols].astype(F32) + nq[part, cols].astype(F32)
            if first == 0:
                total = total + a1[:, cols].astype(F32)
            acc[part, cols] = total * 0.2 - LR * (grad * scale)


def partial_qkv(normed, dqkv, wq, nq, a1):
    width, total = normed.shape
    wide = wq.shape[1]
    return call(
        functools.partial(partial_body, len(dqkv)),
        [(wq.shape, F32)],
        (normed, wq, nq, a1, *dqkv),
        "partial_qkv",
        flops=2 * total * width * wide,
        moved=12 * width * wide,
        vmem=16,
    )[0]


def partial_proj_body(parts, cot, wp, np_, fp, *refs):
    att, acc = refs[:parts], refs[parts]
    scale = wp.shape[0] ** -0.5
    total = wp[...].astype(F32) + np_[...].astype(F32) + fp[...].astype(F32)
    rows, width = att[0].shape[1], wp.shape[1]
    at, grad = 0, 0.0
    for a in att:
        for r in range(0, a.shape[0], width):
            grad = grad + mm(a[r : r + width], cot[at : at + rows], 1, 0)
            at += rows
    acc[...] = total * 0.2 - LR * (grad * scale)


def partial_proj(cot, att, wp, np_, fp):
    total, width = cot.shape
    return call(
        functools.partial(partial_proj_body, len(att)),
        [(wp.shape, F32)],
        (cot, wp, np_, fp, *att),
        "partial_proj",
        flops=2 * total * width * width,
        moved=12 * width * width,
        vmem=16,
        hint=10,
    )[0]


def final_proj_body(acc, s1, out):
    out[...] = (acc[...] + s1[...].astype(F32) * 0.2).astype(BF16)


def final_proj(acc, s1):
    return call(
        final_proj_body,
        [(acc.shape, BF16)],
        (acc, s1),
        "final_proj",
        flops=2 * acc.size,
        moved=8 * acc.size,
        vmem=8,
    )[0]


def chunks(first, last):
    steps = max(1, (last - first) // 96)
    cuts = [first + (last - first) * k // steps // 16 * 16 for k in range(steps)] + [last]
    return list(zip(cuts, cuts[1:]))


def early_body(side, acc, f0, a2, s2, out, token, held, done):
    top, half = a2.shape[0], s2.shape[0]
    copies = []
    for first, last in chunks(0, top) + chunks(top, top + half):
        part = slice(first, last)
        if first < top:
            there = pl.ds(first, last - first)
            late = a2[part]
        else:
            there = pl.ds(pl.multiple_of(first + side[0] * half, 16), last - first)
            late = s2[first - top : last - top]
        late = f0[part].astype(F32) + late.astype(F32)
        held[part] = (acc[there] + late * 0.2).astype(BF16)
        copies.append(pltpu.make_async_copy(held.at[part], out.at[there], done.at[len(copies)]))
        copies[-1].start()
    for copy in copies:
        copy.wait()
    token[...] = jnp.zeros_like(token)


def early_rows(side, acc, f0, a2, s2):
    top, half, wide = a2.shape[0], s2.shape[0], acc.shape[1]
    steps = len(chunks(0, top) + chunks(top, top + half))
    whole = pl.BlockSpec(memory_space=pltpu.VMEM)
    return call(
        early_body,
        [(acc.shape, BF16), ((8, 128), F32)],
        (side, acc, f0, a2, s2),
        "early_rows",
        flops=4 * f0.size,
        moved=10 * f0.size,
        vmem=16,
        in_specs=[pl.BlockSpec(memory_space=pltpu.SMEM)] + [whole] * 4,
        out_specs=[pl.BlockSpec(memory_space=pl.ANY), whole],
        scratch=[pltpu.VMEM((top + half, wide), BF16), pltpu.SemaphoreType.DMA((steps,))],
    )


def last_body(side, acc, f1, other, early, out, held, done):
    half = other.shape[0]
    top = acc.shape[0] - 2 * half
    copies = []
    for first, last in chunks(0, half):
        part = slice(first, last)
        there = pl.ds(pl.multiple_of(top + first + (1 - side[0]) * half, 16), last - first)
        late = f1[part].astype(F32) + other[part].astype(F32)
        held[part] = (acc[there] + late * 0.2).astype(BF16)
        copies.append(pltpu.make_async_copy(held.at[part], out.at[there], done.at[len(copies)]))
        copies[-1].start()
    for copy in copies:
        copy.wait()


def last_rows(side, acc, f1, other, early):
    whole = pl.BlockSpec(memory_space=pltpu.VMEM)
    anywhere = pl.BlockSpec(memory_space=pl.ANY)
    return call(
        last_body,
        [(acc.shape, BF16)],
        (side, acc, f1, other, early),
        "last_rows",
        flops=4 * f1.size,
        moved=10 * f1.size,
        vmem=16,
        in_specs=[pl.BlockSpec(memory_space=pltpu.SMEM)] + [whole] * 3 + [anywhere],
        out_specs=[anywhere],
        scratch=[
            pltpu.VMEM(other.shape, BF16),
            pltpu.SemaphoreType.DMA((len(chunks(0, other.shape[0])),)),
        ],
        aliases={4: 0},
    )[0]


def pair_body(a, b, out):
    out[...] = (a[...].astype(F32) + b[...].astype(F32)).astype(BF16)


def pair_sum(a, b):
    return call(
        pair_body, [(a.shape, BF16)], (a, b), "pair_sum", flops=a.size, moved=6 * a.size, vmem=8
    )[0]


def rows_body(source, out, done):
    pieces = done.shape[0]
    rows = out.shape[0] // pieces
    copies = []
    for k in range(pieces):
        part = pl.ds(k * rows, rows)
        copies.append(pltpu.make_async_copy(source.at[part], out.at[part], done.at[k]))
    for copy in copies:
        copy.start()
    for copy in copies:
        copy.wait()


def first_rows(a, count):
    return call(
        rows_body,
        [((count, a.shape[1]), a.dtype)],
        (a,),
        "first_rows",
        flops=0,
        moved=4 * count * a.shape[1],
        vmem=8,
        in_specs=[pl.BlockSpec(memory_space=pltpu.HBM)],
        scratch=[pltpu.SemaphoreType.DMA((2,))],
    )[0]


def permute(block, axis, partner):
    n = lax.axis_size(axis)
    return lax.ppermute(block, axis, [(i, partner(i, n)) for i in range(n)])


def up(i, n):
    return (i + 1) % n


def down(i, n):
    return (i - 1) % n


def near(i, n):
    return i ^ 1


def far(i, n):
    return (i + 1) % n if i % 2 else (i - 1) % n


def opposite(i, n):
    return i ^ 2


def after(values, *others):
    return lax.optimization_barrier((values, others))[0]


def plain_average(weights, grad):
    total = weights.astype(F32)
    for axis in ("rx", "ry"):
        for partner in (up, down):
            total = total + permute(weights, axis, partner).astype(F32)
    return (total / 5.0 - LR * grad).astype(BF16)


def local(block_input, out_cotangent, w_qkv, w_proj):
    wq, wp = w_qkv[0, 0], w_proj[0, 0]
    images, length, width = block_input.shape[2:]
    rows = -(-length // 16) * 16
    pad = ((0, 0), (0, rows - length), (0, 0))
    tokens = jnp.pad(block_input[0, 0], pad).reshape(images * rows, width)
    cot = jnp.pad(out_cotangent[0, 0], pad).reshape(images * rows, width)
    half = images // 2

    if lax.axis_size("rx") != 4 or lax.axis_size("ry") % 2:
        normed, qkv, datt = project(tokens, cot, wq, wp, rows)
        att, dqkv = attention(qkv, datt, 0, images, rows, length, HEADS)
        scale = width**-0.5
        gq = mm(normed, dqkv, 1, 0) * scale
        gp = jnp.einsum("bdt,bte->de", att.reshape(images, width, rows), cot.reshape(images, rows, width), preferred_element_type=F32) * scale
        return plain_average(wq, gq)[None, None], plain_average(wp, gp)[None, None]

    cut = width * 11 // 24
    part = (width - cut) // 2
    side = lax.axis_index("rx") // 2
    top = first_rows(wq, cut)
    sent = lax.dynamic_slice_in_dim(wq, cut + (1 - side) * part, part)
    kept = lax.dynamic_slice_in_dim(wq, cut + side * part, part)
    b1 = permute(wp, "rx", opposite)
    fp = permute(wp, "ry", far)
    a1 = permute(top, "rx", near)
    nq = permute(wq, "ry", near)
    np_ = permute(wp, "ry", near)
    normed, qkv, datt = project(tokens, cot, wq, wp, rows)

    most = jnp.concatenate([top, kept], axis=0)
    most, sent, qkv, datt = after((most, sent, qkv, datt), nq, np_)
    b2 = permute(sent, "rx", opposite)
    f0 = permute(most, "ry", far)
    att0, dqkv0 = attention(qkv, datt, 0, half, rows, length, HEADS)

    b1, fp = after((b1, fp), att0)
    qkv, datt = after((qkv, datt), b1, fp)
    att1, dqkv1 = attention(qkv, datt, half, images - half, rows, length, HEADS)

    a1, b2 = after(a1, att1), after(b2, att1)
    a2 = permute(a1, "rx", opposite)
    pair2 = pair_sum(kept, b2)
    s2 = permute(pair2, "rx", near)
    dqkv0, dqkv1 = after((dqkv0, dqkv1), pair2)
    acc = partial_qkv(normed, (dqkv0, dqkv1), wq, nq, a1)
    s2 = after(s2, acc)
    other = permute(s2, "rx", opposite)
    pair1 = pair_sum(wp, after(b1, s2))
    s1 = permute(pair1, "rx", near)
    acc_p = partial_proj(cot, after((att0, att1), pair1, a2), wp, np_, fp)
    f1 = permute(after(sent, s2), "ry", far)
    side = side.reshape(1)
    early, token = early_rows(side, acc, f0, a2, s2)
    out_p = final_proj(acc_p, after(s1, token))
    f1, other = after(f1, out_p), after(other, out_p)
    out_q = last_rows(side, acc, f1, other, early)
    return out_q[None, None], out_p[None, None]


def solution(mesh):
    return jax.shard_map(
        local,
        mesh=mesh,
        in_specs=(
            P("rx", "ry", None, None, None),
            P("rx", "ry", None, None, None),
            P("rx", "ry", None, None),
            P("rx", "ry", None, None),
        ),
        out_specs=(P("rx", "ry", None, None), P("rx", "ry", None, None)),
        check_vma=False,
    )
```

```python
import functools

import jax
import jax.numpy as jnp
from jax import lax
from jax.experimental import pallas as pl
from jax.experimental.pallas import tpu as pltpu
from jax.sharding import PartitionSpec as P

HEADS = 12
LR = 1
F32 = jnp.float32
BF16 = jnp.bfloat16
MIB = 2**20


def mm(a, b, ca, cb):
    return lax.dot_general(a, b, (((ca,), (cb,)), ((), ())), preferred_element_type=F32)


def call(body, outs, operands, name, flops, moved, vmem, grid=None, in_specs=None, out_specs=None, scratch=(), exps=0, aliases=None):
    whole = pl.BlockSpec(memory_space=pltpu.VMEM)
    kwargs = {} if grid is None else {"grid": grid}
    return pl.pallas_call(
        body,
        in_specs=in_specs or [whole] * len(operands),
        out_specs=out_specs or [whole] * len(outs),
        out_shape=[jax.ShapeDtypeStruct(shape, dtype) for shape, dtype in outs],
        scratch_shapes=list(scratch),
        compiler_params=pltpu.CompilerParams(vmem_limit_bytes=vmem * MIB),
        cost_estimate=pl.CostEstimate(flops=flops, bytes_accessed=moved, transcendentals=exps),
        input_output_aliases=aliases or {},
        name=name,
        **kwargs,
    )(*operands)


def project_body(rows, tok, cot, wq, wp, turned, qkv, datt, normed):
    c = pl.program_id(0)
    total, width = normed.shape
    scale = width**-0.5

    @pl.when(c == 0)
    def _():
        for r in range(0, total, rows):
            part = slice(r, r + rows)
            x = tok[part].astype(F32)
            xc = x - jnp.mean(x, axis=-1, keepdims=True)
            var = jnp.mean(xc * xc, axis=-1, keepdims=True)
            normed[part] = (xc * lax.rsqrt(var + 1e-06)).astype(BF16)
            datt[part] = (mm(cot[part], wp[...], 1, 1) * scale).astype(BF16)
        turned[...] = normed[...].T

    for r in range(0, total, rows):
        part = slice(r, r + rows)
        qkv[part] = (mm(normed[part], wq[...], 1, 0) * scale).astype(BF16)


def project(tokens, cot, wq, wp, rows):
    total, width = tokens.shape
    fixed = pl.BlockSpec((total, width), lambda c: (0, 0))
    return call(
        functools.partial(project_body, rows),
        [((width, total), BF16), ((total, 3 * width), BF16), ((total, width), BF16)],
        (tokens, cot, wq, wp),
        "project",
        flops=8 * total * width * width,
        moved=16 * total * width + 8 * width * width,
        vmem=32,
        grid=(3,),
        in_specs=[
            fixed,
            fixed,
            pl.BlockSpec((width, width), lambda c: (0, c)),
            pl.BlockSpec((width, width), lambda c: (0, 0)),
        ],
        out_specs=[
            pl.BlockSpec((width, total), lambda c: (0, 0)),
            pl.BlockSpec((total, width), lambda c: (0, c)),
            fixed,
        ],
        scratch=[pltpu.VMEM((total, width), BF16)],
    )


def attention_body(length, heads, unroll, qkv, datt, att, dqkv):
    rows, width = datt.shape
    hd = width // heads
    hscale = hd**-0.5
    pack = 128 // hd
    full = rows // 16 * 16 - 16
    keep = lax.broadcasted_iota(jnp.int32, (rows - full, rows), 0) < length - full
    lane = lax.broadcasted_iota(jnp.int32, (rows, 128), 1)

    def group(g, carry):
        at = [pl.ds(pl.multiple_of(c * width + g * 128, 128), 128) for c in range(3)]
        qg, kg, vg = (qkv[:, a] for a in at)
        dg = datt[:, at[0]]
        kt, vt = kg.T, vg.T
        dk, dv, at_t, dq_t = 0.0, 0.0, [], []
        for j in range(pack):
            own = (lane >= j * hd) & (lane < (j + 1) * hd)
            q = jnp.where(own, qg, jnp.zeros_like(qg)) * jnp.asarray(hscale, BF16)
            da = jnp.where(own, dg, jnp.zeros_like(dg))
            s = mm(kg, q, 1, 1)
            s = jnp.concatenate([s[:full], jnp.where(keep, s[full:], -1e30)], axis=0)
            e = jnp.exp(s - jnp.max(s, axis=0, keepdims=True))
            p = e * (1.0 / jnp.sum(e, axis=0, keepdims=True))
            pb = p.astype(BF16)
            dp = mm(vg, da, 1, 1)
            ds = (p * (dp - jnp.sum(dp * p, axis=0, keepdims=True))).astype(BF16)
            mine = slice(j * hd, (j + 1) * hd)
            at_t.append(mm(vt[mine], pb, 1, 0))
            dq_t.append(mm(kt[mine], ds, 1, 0) * hscale)
            dk = dk + mm(ds, q, 1, 0)
            dv = dv + mm(pb, da, 1, 0)
        att[pl.ds(pl.multiple_of(g * 128, 128), 128), :] = jnp.concatenate(at_t, axis=0).astype(BF16)
        dqkv[:, at[0]] = jnp.concatenate(dq_t, axis=0).astype(BF16).T
        dqkv[:, at[1]] = dk.astype(BF16)
        dqkv[:, at[2]] = dv.astype(BF16)
        return carry

    lax.fori_loop(0, heads // pack, group, 0, unroll=unroll)


def attention(qkv, datt, first, count, rows, length, heads, unroll=6):
    width = datt.shape[1]
    here = lambda b: (b + first, 0)
    there = lambda b: (b, 0)
    return call(
        functools.partial(attention_body, length, heads, unroll),
        [((count * width, rows), BF16), ((count * rows, 3 * width), BF16)],
        (qkv, datt),
        "attention",
        flops=12 * count * rows * 256 * 256 * heads,
        moved=16 * count * rows * width,
        vmem=16,
        grid=(count,),
        in_specs=[pl.BlockSpec((rows, 3 * width), here), pl.BlockSpec((rows, width), here)],
        out_specs=[pl.BlockSpec((width, rows), there), pl.BlockSpec((rows, 3 * width), there)],
        exps=count * heads * rows * rows,
    )


def partial_body(parts, normed, wq, n0, n1, a1, *refs):
    dqkv, acc = refs[:parts], refs[parts]
    rows, wide = wq.shape
    width = wide // 3
    scale = width**-0.5
    for near_rows, first, last in ((n0, 0, a1.shape[0]), (n1, a1.shape[0], rows)):
        part = slice(first, last)
        for c in range(0, wide, width):
            cols = slice(c, c + width)
            at, grad = 0, 0.0
            for d in dqkv:
                grad = grad + mm(normed[part, at : at + d.shape[0]], d[:, cols], 1, 0)
                at += d.shape[0]
            total = wq[part, cols].astype(F32) + near_rows[:, cols].astype(F32)
            if first == 0:
                total = total + a1[:, cols].astype(F32)
            acc[part, cols] = total * 0.2 - LR * (grad * scale)


def partial_qkv(normed, dqkv, wq, n0, n1, a1):
    width, total = normed.shape
    wide = wq.shape[1]
    return call(
        functools.partial(partial_body, len(dqkv)),
        [(wq.shape, F32)],
        (normed, wq, n0, n1, a1, *dqkv),
        "partial_qkv",
        flops=2 * total * width * wide,
        moved=12 * width * wide,
        vmem=16,
    )[0]


def partial_proj_body(parts, cot, wp, np0, np1, fp, *refs):
    att, acc = refs[:parts], refs[parts]
    scale = wp.shape[0] ** -0.5
    near_rows = jnp.concatenate([np0[...], np1[...]], axis=0)
    total = wp[...].astype(F32) + near_rows.astype(F32) + fp[...].astype(F32)
    rows, width = att[0].shape[1], wp.shape[1]
    at, grad = 0, 0.0
    for a in att:
        for r in range(0, a.shape[0], width):
            grad = grad + mm(a[r : r + width], cot[at : at + rows], 1, 0)
            at += rows
    acc[...] = total * 0.2 - LR * (grad * scale)


def partial_proj(cot, att, wp, np0, np1, fp):
    total, width = cot.shape
    return call(
        functools.partial(partial_proj_body, len(att)),
        [(wp.shape, F32)],
        (cot, wp, np0, np1, fp, *att),
        "partial_proj",
        flops=2 * total * width * width,
        moved=12 * width * width,
        vmem=16,
    )[0]


def final_proj_body(acc, s1, out):
    out[...] = (acc[...] + s1[...].astype(F32) * 0.2).astype(BF16)


def final_proj(acc, s1):
    return call(
        final_proj_body,
        [(acc.shape, BF16)],
        (acc, s1),
        "final_proj",
        flops=2 * acc.size,
        moved=8 * acc.size,
        vmem=8,
    )[0]


def chunks(first, last):
    steps = max(1, (last - first) // 96)
    cuts = [first + (last - first) * k // steps // 16 * 16 for k in range(steps)] + [last]
    return list(zip(cuts, cuts[1:]))


def early_body(side, acc, f0, a2, s2, out, token, held, done):
    top, half = a2.shape[0], s2.shape[0]
    copies = []
    for first, last in chunks(0, top) + chunks(top, top + half):
        part = slice(first, last)
        if first < top:
            there = pl.ds(first, last - first)
            late = a2[part]
        else:
            there = pl.ds(pl.multiple_of(first + side[0] * half, 16), last - first)
            late = s2[first - top : last - top]
        late = f0[part].astype(F32) + late.astype(F32)
        held[part] = (acc[there] + late * 0.2).astype(BF16)
        copies.append(pltpu.make_async_copy(held.at[part], out.at[there], done.at[len(copies)]))
        copies[-1].start()
    for copy in copies:
        copy.wait()
    token[...] = jnp.zeros_like(token)


def early_rows(side, acc, f0, a2, s2):
    top, half, wide = a2.shape[0], s2.shape[0], acc.shape[1]
    steps = len(chunks(0, top) + chunks(top, top + half))
    whole = pl.BlockSpec(memory_space=pltpu.VMEM)
    return call(
        early_body,
        [(acc.shape, BF16), ((8, 128), F32)],
        (side, acc, f0, a2, s2),
        "early_rows",
        flops=4 * f0.size,
        moved=10 * f0.size,
        vmem=16,
        in_specs=[pl.BlockSpec(memory_space=pltpu.SMEM)] + [whole] * 4,
        out_specs=[pl.BlockSpec(memory_space=pl.ANY), whole],
        scratch=[pltpu.VMEM((top + half, wide), BF16), pltpu.SemaphoreType.DMA((steps,))],
    )


def last_body(side, acc, f1, other, early, out, held, done):
    half = other.shape[0]
    top = acc.shape[0] - 2 * half
    copies = []
    for first, last in chunks(0, half):
        part = slice(first, last)
        there = pl.ds(pl.multiple_of(top + first + (1 - side[0]) * half, 16), last - first)
        late = f1[part].astype(F32) + other[part].astype(F32)
        held[part] = (acc[there] + late * 0.2).astype(BF16)
        copies.append(pltpu.make_async_copy(held.at[part], out.at[there], done.at[len(copies)]))
        copies[-1].start()
    for copy in copies:
        copy.wait()


def last_rows(side, acc, f1, other, early):
    whole = pl.BlockSpec(memory_space=pltpu.VMEM)
    anywhere = pl.BlockSpec(memory_space=pl.ANY)
    return call(
        last_body,
        [(acc.shape, BF16)],
        (side, acc, f1, other, early),
        "last_rows",
        flops=4 * f1.size,
        moved=10 * f1.size,
        vmem=16,
        in_specs=[pl.BlockSpec(memory_space=pltpu.SMEM)] + [whole] * 3 + [anywhere],
        out_specs=[anywhere],
        scratch=[
            pltpu.VMEM(other.shape, BF16),
            pltpu.SemaphoreType.DMA((len(chunks(0, other.shape[0])),)),
        ],
        aliases={4: 0},
    )[0]


def pair_body(a, b, out):
    out[...] = (a[...].astype(F32) + b[...].astype(F32)).astype(BF16)


def pair_sum(a, b):
    return call(
        pair_body, [(a.shape, BF16)], (a, b), "pair_sum", flops=a.size, moved=6 * a.size, vmem=8
    )[0]


def rows_body(source, out, done):
    pieces = done.shape[0]
    rows = out.shape[0] // pieces
    copies = []
    for k in range(pieces):
        part = pl.ds(k * rows, rows)
        copies.append(pltpu.make_async_copy(source.at[part], out.at[part], done.at[k]))
    for copy in copies:
        copy.start()
    for copy in copies:
        copy.wait()


def first_rows(a, count):
    return call(
        rows_body,
        [((count, a.shape[1]), a.dtype)],
        (a,),
        "first_rows",
        flops=0,
        moved=4 * count * a.shape[1],
        vmem=8,
        in_specs=[pl.BlockSpec(memory_space=pltpu.HBM)],
        scratch=[pltpu.SemaphoreType.DMA((2,))],
    )[0]


def permute(block, axis, partner):
    n = lax.axis_size(axis)
    return lax.ppermute(block, axis, [(i, partner(i, n)) for i in range(n)])


def up(i, n):
    return (i + 1) % n


def down(i, n):
    return (i - 1) % n


def near(i, n):
    return i ^ 1


def far(i, n):
    return (i + 1) % n if i % 2 else (i - 1) % n


def opposite(i, n):
    return i ^ 2


def after(values, *others):
    return lax.optimization_barrier((values, others))[0]


def plain_average(weights, grad):
    total = weights.astype(F32)
    for axis in ("rx", "ry"):
        for partner in (up, down):
            total = total + permute(weights, axis, partner).astype(F32)
    return (total / 5.0 - LR * grad).astype(BF16)


def local(block_input, out_cotangent, w_qkv, w_proj):
    wq, wp = w_qkv[0, 0], w_proj[0, 0]
    images, length, width = block_input.shape[2:]
    rows = -(-length // 16) * 16
    pad = ((0, 0), (0, rows - length), (0, 0))
    tokens = jnp.pad(block_input[0, 0], pad).reshape(images * rows, width)
    cot = jnp.pad(out_cotangent[0, 0], pad).reshape(images * rows, width)
    half = images // 2

    if lax.axis_size("rx") != 4 or lax.axis_size("ry") % 2:
        normed, qkv, datt = project(tokens, cot, wq, wp, rows)
        att, dqkv = attention(qkv, datt, 0, images, rows, length, HEADS)
        scale = width**-0.5
        gq = mm(normed, dqkv, 1, 0) * scale
        gp = jnp.einsum("bdt,bte->de", att.reshape(images, width, rows), cot.reshape(images, rows, width), preferred_element_type=F32) * scale
        return plain_average(wq, gq)[None, None], plain_average(wp, gp)[None, None]

    cut = width * 11 // 24
    part = (width - cut) // 2
    side = lax.axis_index("rx") // 2
    top = first_rows(wq, cut)
    sent = lax.dynamic_slice_in_dim(wq, cut + (1 - side) * part, part)
    kept = lax.dynamic_slice_in_dim(wq, cut + side * part, part)
    b1 = permute(wp, "rx", opposite)
    fp = permute(wp, "ry", far)
    a1 = permute(top, "rx", near)
    normed, qkv, datt = project(tokens, cot, wq, wp, rows)

    most = jnp.concatenate([top, kept], axis=0)
    b2 = permute(sent, "rx", opposite)
    f0 = permute(most, "ry", far)
    att0, dqkv0 = attention(qkv, datt, 0, half, rows, length, HEADS)

    fp, b1 = after((fp, b1), att0)
    qkv, datt, top2, low = after((qkv, datt, top, wq[cut:]), fp, b1)
    n0 = permute(top2, "ry", near)
    n1 = permute(low, "ry", near)
    att1, dqkv1 = attention(qkv, datt, half, images - half, rows, length, HEADS)

    a1, b2 = after(a1, att1), after(b2, att1)
    a2 = permute(a1, "rx", opposite)
    pair2 = pair_sum(kept, b2)
    s2 = permute(pair2, "rx", near)
    wp_top, wp_low = after((wp[: width // 2], wp[width // 2 :]), a2, f0)
    np_ = (permute(wp_top, "ry", near), permute(wp_low, "ry", near))
    s2 = after(s2, n0, n1)
    dqkv0, dqkv1 = after((dqkv0, dqkv1), s2)
    acc = partial_qkv(normed, (dqkv0, dqkv1), wq, n0, n1, a1)
    other = permute(s2, "rx", opposite)
    pair1 = pair_sum(wp, after(b1, s2))
    s1 = permute(pair1, "rx", near)
    acc_p = partial_proj(cot, after((att0, att1), pair1), wp, *np_, fp)
    f1 = permute(after(sent, s2), "ry", far)
    side = side.reshape(1)
    early, token = early_rows(side, acc, f0, a2, s2)
    out_p = final_proj(acc_p, after(s1, token))
    f1, other = after(f1, out_p), after(other, out_p)
    out_q = last_rows(side, acc, f1, other, early)
    return out_q[None, None], out_p[None, None]


def solution(mesh):
    return jax.shard_map(
        local,
        mesh=mesh,
        in_specs=(
            P("rx", "ry", None, None, None),
            P("rx", "ry", None, None, None),
            P("rx", "ry", None, None),
            P("rx", "ry", None, None),
        ),
        out_specs=(P("rx", "ry", None, None), P("rx", "ry", None, None)),
        check_vma=False,
    )
```

```python
import functools

import jax
import jax.numpy as jnp
from jax import lax
from jax.experimental import pallas as pl
from jax.experimental.pallas import tpu as pltpu
from jax.sharding import PartitionSpec as P

HEADS = 12
LR = 1
F32 = jnp.float32
BF16 = jnp.bfloat16
MIB = 2**20


def mm(a, b, ca, cb):
    return lax.dot_general(a, b, (((ca,), (cb,)), ((), ())), preferred_element_type=F32)


def call(body, outs, operands, name, flops, moved, vmem, grid=None, in_specs=None, out_specs=None, scratch=(), exps=0, aliases=None):
    whole = pl.BlockSpec(memory_space=pltpu.VMEM)
    kwargs = {} if grid is None else {"grid": grid}
    return pl.pallas_call(
        body,
        in_specs=in_specs or [whole] * len(operands),
        out_specs=out_specs or [whole] * len(outs),
        out_shape=[jax.ShapeDtypeStruct(shape, dtype) for shape, dtype in outs],
        scratch_shapes=list(scratch),
        compiler_params=pltpu.CompilerParams(vmem_limit_bytes=vmem * MIB),
        cost_estimate=pl.CostEstimate(flops=flops, bytes_accessed=moved, transcendentals=exps),
        input_output_aliases=aliases or {},
        name=name,
        **kwargs,
    )(*operands)


def project_body(rows, tok, cot, wq, wp, turned, qkv, datt, normed):
    c = pl.program_id(0)
    total, width = normed.shape
    scale = width**-0.5

    @pl.when(c == 0)
    def _():
        for r in range(0, total, rows):
            part = slice(r, r + rows)
            x = tok[part].astype(F32)
            xc = x - jnp.mean(x, axis=-1, keepdims=True)
            var = jnp.mean(xc * xc, axis=-1, keepdims=True)
            normed[part] = (xc * lax.rsqrt(var + 1e-06)).astype(BF16)
            datt[part] = (mm(cot[part], wp[...], 1, 1) * scale).astype(BF16)
        turned[...] = normed[...].T

    for r in range(0, total, rows):
        part = slice(r, r + rows)
        qkv[part] = (mm(normed[part], wq[...], 1, 0) * scale).astype(BF16)


def project(tokens, cot, wq, wp, rows):
    total, width = tokens.shape
    fixed = pl.BlockSpec((total, width), lambda c: (0, 0))
    return call(
        functools.partial(project_body, rows),
        [((width, total), BF16), ((total, 3 * width), BF16), ((total, width), BF16)],
        (tokens, cot, wq, wp),
        "project",
        flops=8 * total * width * width,
        moved=16 * total * width + 8 * width * width,
        vmem=32,
        grid=(3,),
        in_specs=[
            fixed,
            fixed,
            pl.BlockSpec((width, width), lambda c: (0, c)),
            pl.BlockSpec((width, width), lambda c: (0, 0)),
        ],
        out_specs=[
            pl.BlockSpec((width, total), lambda c: (0, 0)),
            pl.BlockSpec((total, width), lambda c: (0, c)),
            fixed,
        ],
        scratch=[pltpu.VMEM((total, width), BF16)],
    )


def attention_body(length, heads, unroll, qkv, datt, att, dqkv):
    rows, width = datt.shape
    hd = width // heads
    hscale = hd**-0.5
    pack = 128 // hd
    full = rows // 16 * 16 - 16
    keep = lax.broadcasted_iota(jnp.int32, (rows - full, rows), 0) < length - full
    lane = lax.broadcasted_iota(jnp.int32, (rows, 128), 1)

    def group(g, carry):
        at = [pl.ds(pl.multiple_of(c * width + g * 128, 128), 128) for c in range(3)]
        qg, kg, vg = (qkv[:, a] for a in at)
        dg = datt[:, at[0]]
        kt, vt = kg.T, vg.T
        dk, dv, at_t, dq_t = 0.0, 0.0, [], []
        for j in range(pack):
            own = (lane >= j * hd) & (lane < (j + 1) * hd)
            q = jnp.where(own, qg, jnp.zeros_like(qg)) * jnp.asarray(hscale, BF16)
            da = jnp.where(own, dg, jnp.zeros_like(dg))
            s = mm(kg, q, 1, 1)
            s = jnp.concatenate([s[:full], jnp.where(keep, s[full:], -1e30)], axis=0)
            e = jnp.exp(s - jnp.max(s, axis=0, keepdims=True))
            p = e * (1.0 / jnp.sum(e, axis=0, keepdims=True))
            pb = p.astype(BF16)
            dp = mm(vg, da, 1, 1)
            ds = (p * (dp - jnp.sum(dp * p, axis=0, keepdims=True))).astype(BF16)
            mine = slice(j * hd, (j + 1) * hd)
            at_t.append(mm(vt[mine], pb, 1, 0))
            dq_t.append(mm(kt[mine], ds, 1, 0) * hscale)
            dk = dk + mm(ds, q, 1, 0)
            dv = dv + mm(pb, da, 1, 0)
        att[pl.ds(pl.multiple_of(g * 128, 128), 128), :] = jnp.concatenate(at_t, axis=0).astype(BF16)
        dqkv[:, at[0]] = jnp.concatenate(dq_t, axis=0).astype(BF16).T
        dqkv[:, at[1]] = dk.astype(BF16)
        dqkv[:, at[2]] = dv.astype(BF16)
        return carry

    lax.fori_loop(0, heads // pack, group, 0, unroll=unroll)


def attention(qkv, datt, first, count, rows, length, heads, unroll=6):
    width = datt.shape[1]
    here = lambda b: (b + first, 0)
    there = lambda b: (b, 0)
    return call(
        functools.partial(attention_body, length, heads, unroll),
        [((count * width, rows), BF16), ((count * rows, 3 * width), BF16)],
        (qkv, datt),
        "attention",
        flops=12 * count * rows * 256 * 256 * heads,
        moved=16 * count * rows * width,
        vmem=16,
        grid=(count,),
        in_specs=[pl.BlockSpec((rows, 3 * width), here), pl.BlockSpec((rows, width), here)],
        out_specs=[pl.BlockSpec((width, rows), there), pl.BlockSpec((rows, 3 * width), there)],
        exps=count * heads * rows * rows,
    )


def partial_body(parts, normed, wq, n0, n1, a1, *refs):
    dqkv, acc = refs[:parts], refs[parts]
    rows, wide = wq.shape
    width = wide // 3
    scale = width**-0.5
    for near_rows, first, last in ((n0, 0, a1.shape[0]), (n1, a1.shape[0], rows)):
        part = slice(first, last)
        for c in range(0, wide, width):
            cols = slice(c, c + width)
            at, grad = 0, 0.0
            for d in dqkv:
                grad = grad + mm(normed[part, at : at + d.shape[0]], d[:, cols], 1, 0)
                at += d.shape[0]
            total = wq[part, cols].astype(F32) + near_rows[:, cols].astype(F32)
            if first == 0:
                total = total + a1[:, cols].astype(F32)
            acc[part, cols] = total * 0.2 - LR * (grad * scale)


def partial_qkv(normed, dqkv, wq, n0, n1, a1):
    width, total = normed.shape
    wide = wq.shape[1]
    return call(
        functools.partial(partial_body, len(dqkv)),
        [(wq.shape, F32)],
        (normed, wq, n0, n1, a1, *dqkv),
        "partial_qkv",
        flops=2 * total * width * wide,
        moved=12 * width * wide,
        vmem=16,
    )[0]


def partial_proj_body(parts, cot, wp, np0, np1, fp, *refs):
    att, acc = refs[:parts], refs[parts]
    scale = wp.shape[0] ** -0.5
    near_rows = jnp.concatenate([np0[...], np1[...]], axis=0)
    total = wp[...].astype(F32) + near_rows.astype(F32) + fp[...].astype(F32)
    rows, width = att[0].shape[1], wp.shape[1]
    at, grad = 0, 0.0
    for a in att:
        for r in range(0, a.shape[0], width):
            grad = grad + mm(a[r : r + width], cot[at : at + rows], 1, 0)
            at += rows
    acc[...] = total * 0.2 - LR * (grad * scale)


def partial_proj(cot, att, wp, np0, np1, fp):
    total, width = cot.shape
    return call(
        functools.partial(partial_proj_body, len(att)),
        [(wp.shape, F32)],
        (cot, wp, np0, np1, fp, *att),
        "partial_proj",
        flops=2 * total * width * width,
        moved=12 * width * width,
        vmem=16,
    )[0]


def final_proj_body(acc, s1, out):
    out[...] = (acc[...] + s1[...].astype(F32) * 0.2).astype(BF16)


def final_proj(acc, s1):
    return call(
        final_proj_body,
        [(acc.shape, BF16)],
        (acc, s1),
        "final_proj",
        flops=2 * acc.size,
        moved=8 * acc.size,
        vmem=8,
    )[0]


def chunks(first, last):
    steps = max(1, (last - first) // 48)
    cuts = [first + (last - first) * k // steps // 16 * 16 for k in range(steps)] + [last]
    return list(zip(cuts, cuts[1:]))


def early_body(side, acc, f0, a2, s2, out, token, held, done):
    top, half = a2.shape[0], s2.shape[0]
    copies = []
    for first, last in chunks(0, top) + chunks(top, top + half):
        part = slice(first, last)
        if first < top:
            there = pl.ds(first, last - first)
            late = a2[part]
        else:
            there = pl.ds(pl.multiple_of(first + side[0] * half, 16), last - first)
            late = s2[first - top : last - top]
        late = f0[part].astype(F32) + late.astype(F32)
        held[part] = (acc[there] + late * 0.2).astype(BF16)
        copies.append(pltpu.make_async_copy(held.at[part], out.at[there], done.at[len(copies)]))
        copies[-1].start()
    for copy in copies:
        copy.wait()
    token[...] = jnp.zeros_like(token)


def early_rows(side, acc, f0, a2, s2):
    top, half, wide = a2.shape[0], s2.shape[0], acc.shape[1]
    steps = len(chunks(0, top) + chunks(top, top + half))
    whole = pl.BlockSpec(memory_space=pltpu.VMEM)
    return call(
        early_body,
        [(acc.shape, BF16), ((8, 128), F32)],
        (side, acc, f0, a2, s2),
        "early_rows",
        flops=4 * f0.size,
        moved=10 * f0.size,
        vmem=16,
        in_specs=[pl.BlockSpec(memory_space=pltpu.SMEM)] + [whole] * 4,
        out_specs=[pl.BlockSpec(memory_space=pl.ANY), whole],
        scratch=[pltpu.VMEM((top + half, wide), BF16), pltpu.SemaphoreType.DMA((steps,))],
    )


def last_body(side, acc, f1, other, early, out, held, done):
    half = other.shape[0]
    top = acc.shape[0] - 2 * half
    copies = []
    for first, last in chunks(0, half):
        part = slice(first, last)
        there = pl.ds(pl.multiple_of(top + first + (1 - side[0]) * half, 16), last - first)
        late = f1[part].astype(F32) + other[part].astype(F32)
        held[part] = (acc[there] + late * 0.2).astype(BF16)
        copies.append(pltpu.make_async_copy(held.at[part], out.at[there], done.at[len(copies)]))
        copies[-1].start()
    for copy in copies:
        copy.wait()


def last_rows(side, acc, f1, other, early):
    whole = pl.BlockSpec(memory_space=pltpu.VMEM)
    anywhere = pl.BlockSpec(memory_space=pl.ANY)
    return call(
        last_body,
        [(acc.shape, BF16)],
        (side, acc, f1, other, early),
        "last_rows",
        flops=4 * f1.size,
        moved=10 * f1.size,
        vmem=16,
        in_specs=[pl.BlockSpec(memory_space=pltpu.SMEM)] + [whole] * 3 + [anywhere],
        out_specs=[anywhere],
        scratch=[
            pltpu.VMEM(other.shape, BF16),
            pltpu.SemaphoreType.DMA((len(chunks(0, other.shape[0])),)),
        ],
        aliases={4: 0},
    )[0]


def pair_body(a, b, out):
    out[...] = (a[...].astype(F32) + b[...].astype(F32)).astype(BF16)


def pair_sum(a, b):
    return call(
        pair_body, [(a.shape, BF16)], (a, b), "pair_sum", flops=a.size, moved=6 * a.size, vmem=8
    )[0]


def rows_body(source, out, done):
    pieces = done.shape[0]
    rows = out.shape[0] // pieces
    copies = []
    for k in range(pieces):
        part = pl.ds(k * rows, rows)
        copies.append(pltpu.make_async_copy(source.at[part], out.at[part], done.at[k]))
    for copy in copies:
        copy.start()
    for copy in copies:
        copy.wait()


def first_rows(a, count):
    return call(
        rows_body,
        [((count, a.shape[1]), a.dtype)],
        (a,),
        "first_rows",
        flops=0,
        moved=4 * count * a.shape[1],
        vmem=8,
        in_specs=[pl.BlockSpec(memory_space=pltpu.HBM)],
        scratch=[pltpu.SemaphoreType.DMA((2,))],
    )[0]


def permute(block, axis, partner):
    n = lax.axis_size(axis)
    return lax.ppermute(block, axis, [(i, partner(i, n)) for i in range(n)])


def up(i, n):
    return (i + 1) % n


def down(i, n):
    return (i - 1) % n


def near(i, n):
    return i ^ 1


def far(i, n):
    return (i + 1) % n if i % 2 else (i - 1) % n


def opposite(i, n):
    return i ^ 2


def after(values, *others):
    return lax.optimization_barrier((values, others))[0]


def plain_average(weights, grad):
    total = weights.astype(F32)
    for axis in ("rx", "ry"):
        for partner in (up, down):
            total = total + permute(weights, axis, partner).astype(F32)
    return (total / 5.0 - LR * grad).astype(BF16)


def local(block_input, out_cotangent, w_qkv, w_proj):
    wq, wp = w_qkv[0, 0], w_proj[0, 0]
    images, length, width = block_input.shape[2:]
    rows = -(-length // 16) * 16
    pad = ((0, 0), (0, rows - length), (0, 0))
    tokens = jnp.pad(block_input[0, 0], pad).reshape(images * rows, width)
    cot = jnp.pad(out_cotangent[0, 0], pad).reshape(images * rows, width)
    half = images // 2

    if lax.axis_size("rx") != 4 or lax.axis_size("ry") % 2:
        normed, qkv, datt = project(tokens, cot, wq, wp, rows)
        att, dqkv = attention(qkv, datt, 0, images, rows, length, HEADS)
        scale = width**-0.5
        gq = mm(normed, dqkv, 1, 0) * scale
        gp = jnp.einsum("bdt,bte->de", att.reshape(images, width, rows), cot.reshape(images, rows, width), preferred_element_type=F32) * scale
        return plain_average(wq, gq)[None, None], plain_average(wp, gp)[None, None]

    cut = width // 2
    part = (width - cut) // 2
    side = lax.axis_index("rx") // 2
    top = first_rows(wq, cut)
    sent = lax.dynamic_slice_in_dim(wq, cut + (1 - side) * part, part)
    kept = lax.dynamic_slice_in_dim(wq, cut + side * part, part)
    b1 = permute(wp, "rx", opposite)
    fp = permute(wp, "ry", far)
    a1 = permute(top, "rx", near)
    normed, qkv, datt = project(tokens, cot, wq, wp, rows)

    most = jnp.concatenate([top, kept], axis=0)
    b2 = permute(sent, "rx", opposite)
    f0 = permute(most, "ry", far)
    att0, dqkv0 = attention(qkv, datt, 0, half, rows, length, HEADS)

    fp, b1 = after((fp, b1), att0)
    qkv, datt, top2, low = after((qkv, datt, top, wq[cut:]), fp, b1)
    n0 = permute(top2, "ry", near)
    n1 = permute(low, "ry", near)
    att1, dqkv1 = attention(qkv, datt, half, images - half, rows, length, HEADS)

    a1, b2 = after(a1, att1), after(b2, att1)
    a2 = permute(a1, "rx", opposite)
    pair2 = pair_sum(kept, b2)
    s2 = permute(pair2, "rx", near)
    wp_top, wp_low = after((wp[: width // 2], wp[width // 2 :]), a2, f0)
    np_ = (permute(wp_top, "ry", near), permute(wp_low, "ry", near))
    s2 = after(s2, n0, n1)
    dqkv0, dqkv1 = after((dqkv0, dqkv1), s2)
    acc = partial_qkv(normed, (dqkv0, dqkv1), wq, n0, n1, a1)
    other = permute(s2, "rx", opposite)
    pair1 = pair_sum(wp, after(b1, s2))
    s1 = permute(pair1, "rx", near)
    acc_p = partial_proj(cot, after((att0, att1), pair1), wp, *np_, fp)
    f1 = permute(after(sent, s2), "ry", far)
    side = side.reshape(1)
    early, token = early_rows(side, acc, f0, a2, s2)
    out_p = final_proj(acc_p, after(s1, token))
    f1, other = after(f1, out_p), after(other, out_p)
    out_q = last_rows(side, acc, f1, other, early)
    return out_q[None, None], out_p[None, None]


def solution(mesh):
    return jax.shard_map(
        local,
        mesh=mesh,
        in_specs=(
            P("rx", "ry", None, None, None),
            P("rx", "ry", None, None, None),
            P("rx", "ry", None, None),
            P("rx", "ry", None, None),
        ),
        out_specs=(P("rx", "ry", None, None), P("rx", "ry", None, None)),
        check_vma=False,
    )
```

```python
import functools

import jax
import jax.numpy as jnp
from jax import lax
from jax.experimental import pallas as pl
from jax.experimental.pallas import tpu as pltpu
from jax.sharding import PartitionSpec as P

HEADS = 12
LR = 1
F32 = jnp.float32
BF16 = jnp.bfloat16
MIB = 2**20


def mm(a, b, ca, cb):
    return lax.dot_general(a, b, (((ca,), (cb,)), ((), ())), preferred_element_type=F32)


def call(body, outs, operands, name, flops, moved, vmem, grid=None, in_specs=None, out_specs=None, scratch=(), exps=0, aliases=None):
    whole = pl.BlockSpec(memory_space=pltpu.VMEM)
    kwargs = {} if grid is None else {"grid": grid}
    return pl.pallas_call(
        body,
        in_specs=in_specs or [whole] * len(operands),
        out_specs=out_specs or [whole] * len(outs),
        out_shape=[jax.ShapeDtypeStruct(shape, dtype) for shape, dtype in outs],
        scratch_shapes=list(scratch),
        compiler_params=pltpu.CompilerParams(vmem_limit_bytes=vmem * MIB),
        cost_estimate=pl.CostEstimate(flops=flops, bytes_accessed=moved, transcendentals=exps),
        input_output_aliases=aliases or {},
        name=name,
        **kwargs,
    )(*operands)


def project_body(rows, tok, cot, wq, wp, turned, qkv, datt, normed):
    c = pl.program_id(0)
    total, width = normed.shape
    scale = width**-0.5

    @pl.when(c == 0)
    def _():
        for r in range(0, total, rows):
            part = slice(r, r + rows)
            x = tok[part].astype(F32)
            xc = x - jnp.mean(x, axis=-1, keepdims=True)
            var = jnp.mean(xc * xc, axis=-1, keepdims=True)
            normed[part] = (xc * lax.rsqrt(var + 1e-06)).astype(BF16)
            datt[part] = (mm(cot[part], wp[...], 1, 1) * scale).astype(BF16)
        turned[...] = normed[...].T

    for r in range(0, total, rows):
        part = slice(r, r + rows)
        qkv[part] = (mm(normed[part], wq[...], 1, 0) * scale).astype(BF16)


def project(tokens, cot, wq, wp, rows):
    total, width = tokens.shape
    fixed = pl.BlockSpec((total, width), lambda c: (0, 0))
    return call(
        functools.partial(project_body, rows),
        [((width, total), BF16), ((total, 3 * width), BF16), ((total, width), BF16)],
        (tokens, cot, wq, wp),
        "project",
        flops=8 * total * width * width,
        moved=16 * total * width + 8 * width * width,
        vmem=32,
        grid=(3,),
        in_specs=[
            fixed,
            fixed,
            pl.BlockSpec((width, width), lambda c: (0, c)),
            pl.BlockSpec((width, width), lambda c: (0, 0)),
        ],
        out_specs=[
            pl.BlockSpec((width, total), lambda c: (0, 0)),
            pl.BlockSpec((total, width), lambda c: (0, c)),
            fixed,
        ],
        scratch=[pltpu.VMEM((total, width), BF16)],
    )


def attention_body(length, heads, unroll, qkv, datt, att, dqkv):
    rows, width = datt.shape
    hd = width // heads
    hscale = hd**-0.5
    pack = 128 // hd
    full = rows // 16 * 16 - 16
    keep = lax.broadcasted_iota(jnp.int32, (rows - full, rows), 0) < length - full
    lane = lax.broadcasted_iota(jnp.int32, (rows, 128), 1)

    def group(g, carry):
        at = [pl.ds(pl.multiple_of(c * width + g * 128, 128), 128) for c in range(3)]
        qg, kg, vg = (qkv[:, a] for a in at)
        dg = datt[:, at[0]]
        kt, vt = kg.T, vg.T
        dk, dv, at_t, dq_t = 0.0, 0.0, [], []
        for j in range(pack):
            own = (lane >= j * hd) & (lane < (j + 1) * hd)
            q = jnp.where(own, qg, jnp.zeros_like(qg)) * jnp.asarray(hscale, BF16)
            da = jnp.where(own, dg, jnp.zeros_like(dg))
            s = mm(kg, q, 1, 1)
            s = jnp.concatenate([s[:full], jnp.where(keep, s[full:], -1e30)], axis=0)
            e = jnp.exp(s - jnp.max(s, axis=0, keepdims=True))
            p = e * (1.0 / jnp.sum(e, axis=0, keepdims=True))
            pb = p.astype(BF16)
            dp = mm(vg, da, 1, 1)
            ds = (p * (dp - jnp.sum(dp * p, axis=0, keepdims=True))).astype(BF16)
            mine = slice(j * hd, (j + 1) * hd)
            at_t.append(mm(vt[mine], pb, 1, 0))
            dq_t.append(mm(kt[mine], ds, 1, 0) * hscale)
            dk = dk + mm(ds, q, 1, 0)
            dv = dv + mm(pb, da, 1, 0)
        att[pl.ds(pl.multiple_of(g * 128, 128), 128), :] = jnp.concatenate(at_t, axis=0).astype(BF16)
        dqkv[:, at[0]] = jnp.concatenate(dq_t, axis=0).astype(BF16).T
        dqkv[:, at[1]] = dk.astype(BF16)
        dqkv[:, at[2]] = dv.astype(BF16)
        return carry

    lax.fori_loop(0, heads // pack, group, 0, unroll=unroll)


def attention(qkv, datt, first, count, rows, length, heads, unroll=6):
    width = datt.shape[1]
    here = lambda b: (b + first, 0)
    there = lambda b: (b, 0)
    return call(
        functools.partial(attention_body, length, heads, unroll),
        [((count * width, rows), BF16), ((count * rows, 3 * width), BF16)],
        (qkv, datt),
        "attention",
        flops=12 * count * rows * 256 * 256 * heads,
        moved=16 * count * rows * width,
        vmem=16,
        grid=(count,),
        in_specs=[pl.BlockSpec((rows, 3 * width), here), pl.BlockSpec((rows, width), here)],
        out_specs=[pl.BlockSpec((width, rows), there), pl.BlockSpec((rows, 3 * width), there)],
        exps=count * heads * rows * rows,
    )


def partial_body(parts, normed, wq, n0, n1, a1, *refs):
    dqkv, acc = refs[:parts], refs[parts]
    rows, wide = wq.shape
    width = wide // 3
    scale = width**-0.5
    for near_rows, first, last in ((n0, 0, a1.shape[0]), (n1, a1.shape[0], rows)):
        part = slice(first, last)
        for c in range(0, wide, width):
            cols = slice(c, c + width)
            at, grad = 0, 0.0
            for d in dqkv:
                grad = grad + mm(normed[part, at : at + d.shape[0]], d[:, cols], 1, 0)
                at += d.shape[0]
            total = wq[part, cols].astype(F32) + near_rows[:, cols].astype(F32)
            if first == 0:
                total = total + a1[:, cols].astype(F32)
            acc[part, cols] = total * 0.2 - LR * (grad * scale)


def partial_qkv(normed, dqkv, wq, n0, n1, a1):
    width, total = normed.shape
    wide = wq.shape[1]
    return call(
        functools.partial(partial_body, len(dqkv)),
        [(wq.shape, F32)],
        (normed, wq, n0, n1, a1, *dqkv),
        "partial_qkv",
        flops=2 * total * width * wide,
        moved=12 * width * wide,
        vmem=16,
    )[0]


def partial_proj_body(parts, cot, wp, np0, np1, fp, *refs):
    att, acc = refs[:parts], refs[parts]
    scale = wp.shape[0] ** -0.5
    near_rows = jnp.concatenate([np0[...], np1[...]], axis=0)
    total = wp[...].astype(F32) + near_rows.astype(F32) + fp[...].astype(F32)
    rows, width = att[0].shape[1], wp.shape[1]
    at, grad = 0, 0.0
    for a in att:
        for r in range(0, a.shape[0], width):
            grad = grad + mm(a[r : r + width], cot[at : at + rows], 1, 0)
            at += rows
    acc[...] = total * 0.2 - LR * (grad * scale)


def partial_proj(cot, att, wp, np0, np1, fp):
    total, width = cot.shape
    return call(
        functools.partial(partial_proj_body, len(att)),
        [(wp.shape, F32)],
        (cot, wp, np0, np1, fp, *att),
        "partial_proj",
        flops=2 * total * width * width,
        moved=12 * width * width,
        vmem=16,
    )[0]


def final_proj_body(acc, s1, out):
    out[...] = (acc[...] + s1[...].astype(F32) * 0.2).astype(BF16)


def final_proj(acc, s1):
    return call(
        final_proj_body,
        [(acc.shape, BF16)],
        (acc, s1),
        "final_proj",
        flops=2 * acc.size,
        moved=8 * acc.size,
        vmem=8,
    )[0]


def chunks(first, last):
    steps = max(1, (last - first) // 32)
    cuts = [first + (last - first) * k // steps // 16 * 16 for k in range(steps)] + [last]
    return list(zip(cuts, cuts[1:]))


def early_body(side, acc, f0, a2, s2, out, token, held, done):
    top, half = a2.shape[0], s2.shape[0]
    copies = []
    for first, last in chunks(0, top) + chunks(top, top + half):
        part = slice(first, last)
        if first < top:
            there = pl.ds(first, last - first)
            late = a2[part]
        else:
            there = pl.ds(pl.multiple_of(first + side[0] * half, 16), last - first)
            late = s2[first - top : last - top]
        late = f0[part].astype(F32) + late.astype(F32)
        held[part] = (acc[there] + late * 0.2).astype(BF16)
        copies.append(pltpu.make_async_copy(held.at[part], out.at[there], done.at[len(copies)]))
        copies[-1].start()
    for copy in copies:
        copy.wait()
    token[...] = jnp.zeros_like(token)


def early_rows(side, acc, f0, a2, s2):
    top, half, wide = a2.shape[0], s2.shape[0], acc.shape[1]
    steps = len(chunks(0, top) + chunks(top, top + half))
    whole = pl.BlockSpec(memory_space=pltpu.VMEM)
    return call(
        early_body,
        [(acc.shape, BF16), ((8, 128), F32)],
        (side, acc, f0, a2, s2),
        "early_rows",
        flops=4 * f0.size,
        moved=10 * f0.size,
        vmem=16,
        in_specs=[pl.BlockSpec(memory_space=pltpu.SMEM)] + [whole] * 4,
        out_specs=[pl.BlockSpec(memory_space=pl.ANY), whole],
        scratch=[pltpu.VMEM((top + half, wide), BF16), pltpu.SemaphoreType.DMA((steps,))],
    )


def last_body(side, acc, f1, other, early, out, held, done):
    half = other.shape[0]
    top = acc.shape[0] - 2 * half
    copies = []
    for first, last in chunks(0, half):
        part = slice(first, last)
        there = pl.ds(pl.multiple_of(top + first + (1 - side[0]) * half, 16), last - first)
        late = f1[part].astype(F32) + other[part].astype(F32)
        held[part] = (acc[there] + late * 0.2).astype(BF16)
        copies.append(pltpu.make_async_copy(held.at[part], out.at[there], done.at[len(copies)]))
        copies[-1].start()
    for copy in copies:
        copy.wait()


def last_rows(side, acc, f1, other, early):
    whole = pl.BlockSpec(memory_space=pltpu.VMEM)
    anywhere = pl.BlockSpec(memory_space=pl.ANY)
    return call(
        last_body,
        [(acc.shape, BF16)],
        (side, acc, f1, other, early),
        "last_rows",
        flops=4 * f1.size,
        moved=10 * f1.size,
        vmem=16,
        in_specs=[pl.BlockSpec(memory_space=pltpu.SMEM)] + [whole] * 3 + [anywhere],
        out_specs=[anywhere],
        scratch=[
            pltpu.VMEM(other.shape, BF16),
            pltpu.SemaphoreType.DMA((len(chunks(0, other.shape[0])),)),
        ],
        aliases={4: 0},
    )[0]


def pair_body(a, b, out):
    out[...] = (a[...].astype(F32) + b[...].astype(F32)).astype(BF16)


def pair_sum(a, b):
    return call(
        pair_body, [(a.shape, BF16)], (a, b), "pair_sum", flops=a.size, moved=6 * a.size, vmem=8
    )[0]


def rows_body(source, out, done):
    pieces = done.shape[0]
    rows = out.shape[0] // pieces
    copies = []
    for k in range(pieces):
        part = pl.ds(k * rows, rows)
        copies.append(pltpu.make_async_copy(source.at[part], out.at[part], done.at[k]))
    for copy in copies:
        copy.start()
    for copy in copies:
        copy.wait()


def first_rows(a, count):
    return call(
        rows_body,
        [((count, a.shape[1]), a.dtype)],
        (a,),
        "first_rows",
        flops=0,
        moved=4 * count * a.shape[1],
        vmem=8,
        in_specs=[pl.BlockSpec(memory_space=pltpu.HBM)],
        scratch=[pltpu.SemaphoreType.DMA((2,))],
    )[0]


def permute(block, axis, partner):
    n = lax.axis_size(axis)
    return lax.ppermute(block, axis, [(i, partner(i, n)) for i in range(n)])


def up(i, n):
    return (i + 1) % n


def down(i, n):
    return (i - 1) % n


def near(i, n):
    return i ^ 1


def far(i, n):
    return (i + 1) % n if i % 2 else (i - 1) % n


def opposite(i, n):
    return i ^ 2


def after(values, *others):
    return lax.optimization_barrier((values, others))[0]


def plain_average(weights, grad):
    total = weights.astype(F32)
    for axis in ("rx", "ry"):
        for partner in (up, down):
            total = total + permute(weights, axis, partner).astype(F32)
    return (total / 5.0 - LR * grad).astype(BF16)


def local(block_input, out_cotangent, w_qkv, w_proj):
    wq, wp = w_qkv[0, 0], w_proj[0, 0]
    images, length, width = block_input.shape[2:]
    rows = -(-length // 16) * 16
    pad = ((0, 0), (0, rows - length), (0, 0))
    tokens = jnp.pad(block_input[0, 0], pad).reshape(images * rows, width)
    cot = jnp.pad(out_cotangent[0, 0], pad).reshape(images * rows, width)
    half = images // 2

    if lax.axis_size("rx") != 4 or lax.axis_size("ry") % 2:
        normed, qkv, datt = project(tokens, cot, wq, wp, rows)
        att, dqkv = attention(qkv, datt, 0, images, rows, length, HEADS)
        scale = width**-0.5
        gq = mm(normed, dqkv, 1, 0) * scale
        gp = jnp.einsum("bdt,bte->de", att.reshape(images, width, rows), cot.reshape(images, rows, width), preferred_element_type=F32) * scale
        return plain_average(wq, gq)[None, None], plain_average(wp, gp)[None, None]

    cut = width // 2
    part = (width - cut) // 2
    side = lax.axis_index("rx") // 2
    top = first_rows(wq, cut)
    sent = lax.dynamic_slice_in_dim(wq, cut + (1 - side) * part, part)
    kept = lax.dynamic_slice_in_dim(wq, cut + side * part, part)
    b1 = permute(wp, "rx", opposite)
    fp = permute(wp, "ry", far)
    a1 = permute(top, "rx", near)
    normed, qkv, datt = project(tokens, cot, wq, wp, rows)

    most = jnp.concatenate([top, kept], axis=0)
    b2 = permute(sent, "rx", opposite)
    f0 = permute(most, "ry", far)
    att0, dqkv0 = attention(qkv, datt, 0, half, rows, length, HEADS)

    fp, b1 = after((fp, b1), att0)
    qkv, datt, top2, low = after((qkv, datt, top, wq[cut:]), fp, b1)
    n0 = permute(top2, "ry", near)
    n1 = permute(low, "ry", near)
    att1, dqkv1 = attention(qkv, datt, half, images - half, rows, length, HEADS)

    a1, b2 = after(a1, att1), after(b2, att1)
    a2 = permute(a1, "rx", opposite)
    pair2 = pair_sum(kept, b2)
    s2 = permute(pair2, "rx", near)
    wp_top, wp_low = after((wp[: width // 2], wp[width // 2 :]), a2, f0)
    np_ = (permute(wp_top, "ry", near), permute(wp_low, "ry", near))
    s2 = after(s2, n0, n1)
    dqkv0, dqkv1 = after((dqkv0, dqkv1), s2)
    acc = partial_qkv(normed, (dqkv0, dqkv1), wq, n0, n1, a1)
    other = permute(s2, "rx", opposite)
    pair1 = pair_sum(wp, after(b1, s2))
    s1 = permute(pair1, "rx", near)
    acc_p = partial_proj(cot, after((att0, att1), pair1), wp, *np_, fp)
    f1 = permute(after(sent, s2), "ry", far)
    side = side.reshape(1)
    early, token = early_rows(side, acc, f0, a2, s2)
    out_p = final_proj(acc_p, after(s1, token))
    f1, other = after(f1, out_p), after(other, out_p)
    out_q = last_rows(side, acc, f1, other, early)
    return out_q[None, None], out_p[None, None]


def solution(mesh):
    return jax.shard_map(
        local,
        mesh=mesh,
        in_specs=(
            P("rx", "ry", None, None, None),
            P("rx", "ry", None, None, None),
            P("rx", "ry", None, None),
            P("rx", "ry", None, None),
        ),
        out_specs=(P("rx", "ry", None, None), P("rx", "ry", None, None)),
        check_vma=False,
    )
```
